256 devices in a mesh: vocab: 128 (over y, x, z), rows: 2 (over core).
Axes of the slice: x: 4, y: 4, z: 8, core: 2. Of those that a mesh axis runs over, the one named last changes fastest.
Arguments:
- hidden: bfloat16 [512, 4096], P('rows', 'vocab'), may hold values from -64 to 64
- head_weight: bfloat16 [4096, 131072], P(None, 'vocab'), may hold values from -0.09375 to 0.09375
- mentor_outputs: bfloat16 [512, 131072], P('rows', 'vocab'), may hold values from -480 to 480
Outputs:
- hidden_grad: bfloat16 [512, 4096], P('rows', 'vocab')
- weight_grad: bfloat16 [4096, 131072], P('rows', 'vocab')
- per_position_mismatch: float32 [512], P('rows')
The draws below stay inside these ranges and needn't reach their ends.
All inputs are finite; a program needn't handle non-finite values.
Results may differ from the reference program's by a relative error of at most 0.0043.
Values may be sent and summed in bfloat16 or wider, within the bound.
No kernel may reach another device: no remote copies, remote signals or barrier semaphores. Data moves between devices by JAX's collectives and lax.ppermute only.
A program may use at most 128 MiB of HBM per device.

```python
import math
import jax
import jax.numpy as jnp

D = 4096
VOCAB = 131072
TOKENS = 512


def draw_hidden(key, part):
    key = jax.random.fold_in(key, 11)
    first, second = jax.random.split(key, 2)
    base = jnp.clip(jax.random.normal(first, (TOKENS, D), jnp.float32), -6.0, 6.0)
    scale = jnp.exp(jax.random.uniform(second, (TOKENS, 1), jnp.float32, 0.0, math.log(10.0)))
    return jnp.clip(base * scale, -64.0, 64.0).astype(jnp.bfloat16)


def draw_mentor_outputs(key, part):
    key = jax.random.fold_in(key, 12)
    first, second, third = jax.random.split(key, 3)
    column = jnp.arange(VOCAB, dtype=jnp.float32)[None, :] / VOCAB
    column_scale = (1.0 + 2.0 * column) * jnp.exp(jax.random.uniform(third, (1, VOCAB), jnp.float32, 0.0, math.log(2.0)))
    base = jnp.clip(jax.random.normal(first, (TOKENS, VOCAB), jnp.float32), -5.0, 5.0)
    scale = jnp.exp(jax.random.uniform(second, (TOKENS, 1), jnp.float32, 0.0, math.log(10.0)))
    return jnp.clip(base * scale * column_scale, -480.0, 480.0).astype(jnp.bfloat16)


def block_levels(own_key, shape, shards, smallest, high):
    gain, own = 1.0, jax.random.fold_in(own_key, 6)
    for position, parts in shards:
        draws = jnp.exp(jax.random.uniform(jax.random.fold_in(own, position), (parts,), jnp.float32, smallest / len(shards), high / len(shards)))
        gain = gain * jnp.repeat(draws, shape[position] // parts).reshape([-1 if axis == position else 1 for axis in range(len(shape))])
    return gain


def noise(own_key, dims, scale, bound, pieces=(), held_as=jnp.bfloat16):
    drawn = jax.random.normal(own_key, dims, jnp.float32) * scale
    if len(pieces) > 0:
        drawn = block_levels(own_key, dims, pieces, -0.22, 0.18) * drawn
    return jnp.clip(drawn, min=-bound, max=bound).astype(held_as)


def setup_inputs(seed: int = 0) -> dict:
    key_list = jax.random.split(jax.random.key(seed), 4)
    return {
        "hidden": draw_hidden(jax.random.fold_in(key_list[3], 71), 0),
        "head_weight": noise(key_list[1], (D, VOCAB), D ** -0.5, 0.09375, ((1, 128),)),
        "mentor_outputs": draw_mentor_outputs(jax.random.fold_in(key_list[3], 71), 0),
    }


sharpness_divisor = 2.0
objective_factor = 32.0


def reference(hidden, head_weight, mentor_outputs):
    unnormalized_outputs = jnp.dot(hidden, head_weight, preferred_element_type=jnp.float32)
    learner_raw_outputs = unnormalized_outputs / sharpness_divisor
    mentor_raw_outputs = mentor_outputs.astype(jnp.float32) / sharpness_divisor
    learner_partition_value = jax.nn.logsumexp(learner_raw_outputs, axis=1, keepdims=True)
    mentor_partition_value = jax.nn.logsumexp(mentor_raw_outputs, axis=1, keepdims=True)
    learner_likelihood = jnp.exp(learner_raw_outputs - learner_partition_value)
    mentor_likelihood = jnp.exp(mentor_raw_outputs - mentor_partition_value)
    mismatch_summand = jnp.sum(mentor_likelihood * (mentor_raw_outputs - learner_raw_outputs), axis=1)
    per_position_mismatch = sharpness_divisor * sharpness_divisor * (mismatch_summand + learner_partition_value[:, 0] - mentor_partition_value[:, 0])
    raw_score_derivative = (objective_factor * sharpness_divisor * (learner_likelihood - mentor_likelihood)).astype(jnp.bfloat16)
    hidden_grad = jnp.dot(raw_score_derivative, head_weight.T, preferred_element_type=jnp.float32).astype(jnp.bfloat16)
    weight_grad = jnp.dot(hidden.T, raw_score_derivative, preferred_element_type=jnp.float32).astype(jnp.bfloat16)
    return hidden_grad, weight_grad, per_position_mismatch
```

```python
import jax
import jax.numpy as jnp
from jax import lax
from jax.sharding import PartitionSpec as P

sharpness_divisor = 2.0
objective_factor = 32.0

NY, NX, NZ = 4, 4, 8


def place(y, x, z):
    return (y * NX + x) * NZ + z


z_groups = [[place(y, x, z) for z in range(NZ)] for y in range(NY) for x in range(NX)]
xy_groups = [[place(y, x, z) for y in range(NY) for x in range(NX)] for z in range(NZ)]


def trade(chunks, groups):
    return lax.all_to_all(chunks, "vocab", 0, 0, tiled=True, axis_index_groups=groups)


def spread(block, count, groups):
    return trade(jnp.broadcast_to(block[None], (count,) + block.shape), groups)


def other_core(value):
    return lax.ppermute(value, "rows", [(0, 1), (1, 0)])


def local_lse(scores):
    top = jnp.max(scores, axis=1)
    return top + jnp.log(jnp.sum(jnp.exp(scores - top[:, None]), axis=1))


def lse_of_shards(parts):
    top = jnp.max(parts, axis=0)
    return top + jnp.log(jnp.sum(jnp.exp(parts - top[None]), axis=0))


def shards(hidden, head_weight, mentor_outputs):
    core = lax.axis_index("rows")
    slab = spread(hidden.T, NZ, z_groups).reshape(256, 256)
    hidden_t = spread(slab, NX * NY, xy_groups).reshape(4096, 256)
    mine = lax.dynamic_slice_in_dim(hidden_t, core * 2048, 2048, 0)
    theirs = other_core(lax.dynamic_slice_in_dim(hidden_t, (1 - core) * 2048, 2048, 0))

    target = mentor_outputs.astype(jnp.float32) / sharpness_divisor
    lse_t = local_lse(target)
    student = (
        lax.dot_general(
            hidden_t, head_weight, (((0,), (0,)), ((), ())), preferred_element_type=jnp.float32
        )
        / sharpness_divisor
    )
    lse_s = local_lse(student)
    cross = jnp.sum(jnp.exp(target - lse_t[:, None]) * (target - student), axis=1)
    stats = jnp.stack([lse_s, lse_t, cross]).reshape(6, 128)
    stats = spread(stats, NX * NY * NZ, None).reshape(128, 3, 256)
    all_s, all_t = lse_of_shards(stats[:, 0]), lse_of_shards(stats[:, 1])
    all_cross = jnp.sum(jnp.exp(stats[:, 1] - all_t[None]) * stats[:, 2], axis=0)
    mismatch = sharpness_divisor * sharpness_divisor * (all_cross + all_s - all_t)

    score = (
        objective_factor
        * sharpness_divisor
        * (jnp.exp(student - all_s[:, None]) - jnp.exp(target - all_t[:, None]))
    ).astype(jnp.bfloat16)
    score_theirs = other_core(score)

    part = lax.dot_general(
        head_weight, score, (((1,), (1,)), ((), ())), preferred_element_type=jnp.float32
    ).astype(jnp.bfloat16)
    part = trade(part.reshape(16, 256, 256), xy_groups)
    part = jnp.sum(part.astype(jnp.float32), axis=0).astype(jnp.bfloat16)
    part = trade(part.reshape(8, 32, 256), z_groups)
    hidden_grad = jnp.sum(part.astype(jnp.float32), axis=0).astype(jnp.bfloat16).T

    weight_grad = jnp.dot(
        jnp.concatenate([mine, theirs], axis=1),
        jnp.concatenate([score, score_theirs], axis=0),
        preferred_element_type=jnp.float32,
    ).astype(jnp.bfloat16)
    return (hidden_grad, weight_grad, mismatch)


def solution(mesh):
    return jax.shard_map(
        shards,
        mesh=mesh,
        in_specs=(P("rows", "vocab"), P(None, "vocab"), P("rows", "vocab")),
        out_specs=(P("rows", "vocab"), P("rows", "vocab"), P("rows")),
        check_vma=False,
    )
```

```python
import functools

import jax
import jax.numpy as jnp
from jax import lax
from jax.experimental import pallas as pl
from jax.experimental.pallas import tpu as pltpu
from jax.sharding import PartitionSpec as P

sharpness_divisor = 2.0
objective_factor = 32.0

NY, NX, NZ = 4, 4, 8
ROWS, FULL, COLS, SLAB = 256, 4096, 1024, 256
f32, bf16 = jnp.float32, jnp.bfloat16
MIB = 1 << 20


def place(y, x, z):
    return ((y % NY) * NX + x % NX) * NZ + z % NZ


class_groups = [
    [place(y, c - 2 * y, z) for y in range(NY) for z in range(NZ)] for c in range(4)
]


def trade(chunks, groups):
    return lax.all_to_all(chunks, "vocab", 0, 0, tiled=True, axis_index_groups=groups)


def step(value, dy, dx):
    pairs = [
        (place(y, x, z), place(y + dy, x + dx, z))
        for y in range(NY)
        for x in range(NX)
        for z in range(NZ)
    ]
    return lax.ppermute(value, "vocab", pairs)


def other_core(value):
    return lax.ppermute(value, "rows", [(0, 1), (1, 0)])


def slab_row(own, offset, j):
    slab = 4 * j + lax.rem(own + offset - 2 * j + 8, 4)
    return pl.multiple_of(slab * SLAB, SLAB)


def call(body, outs, ins, flops, traffic, scratch=(), limit=32):
    smem, vmem, hbm = pltpu.SMEM, pltpu.VMEM, pl.ANY
    spaces = {"s": smem, "v": vmem, "h": hbm}
    return pl.pallas_call(
        body,
        out_shape=[jax.ShapeDtypeStruct(shape, dtype) for shape, dtype in outs],
        in_specs=[pl.BlockSpec(memory_space=spaces[kind]) for kind, _ in ins],
        out_specs=[pl.BlockSpec(memory_space=vmem) for _ in outs],
        scratch_shapes=list(scratch),
        compiler_params=pltpu.CompilerParams(vmem_limit_bytes=limit * MIB),
        cost_estimate=pl.CostEstimate(flops=flops, bytes_accessed=traffic, transcendentals=0),
    )(*[value for _, value in ins])


def target_kernel(mentor, prob, lse):
    target = mentor[...].astype(f32) / sharpness_divisor
    top = jnp.max(target, axis=1, keepdims=True)
    value = top + jnp.log(jnp.sum(jnp.exp(target - top), axis=1, keepdims=True))
    prob[...] = jnp.exp(target - value)
    lse[...] = jnp.broadcast_to(value, lse.shape)


def student_kernel(own, a, b, c, d0, d1, head, mentor, prob, lse_t, student, stats, held, sems):
    pieces = [(0, [a.at[pl.ds(j * SLAB, SLAB)] for j in range(4)])]
    pieces.append((1, [b.at[pl.ds(j * SLAB, SLAB)] for j in range(4)]))
    pieces.append((3, [c.at[pl.ds(j * SLAB, SLAB)] for j in range(4)]))
    pieces.append((2, [d.at[pl.ds(j * SLAB, SLAB)] for d in (d0, d1) for j in range(2)]))
    slabs = [(offset, j, ref) for offset, refs in pieces for j, ref in enumerate(refs)]

    def fetch(k):
        offset, j, _ = slabs[k]
        rows = pl.ds(slab_row(own[0], offset, j), SLAB)
        return pltpu.make_async_copy(head.at[rows], held.at[k], sems.at[k])

    for k in range(16):
        fetch(k).start()
    for k in range(16):
        fetch(k).wait()
        product = lax.dot_general(
            slabs[k][2][...], held[k], (((0,), (0,)), ((), ())), preferred_element_type=f32
        )
        if k == 0:
            student[...] = product
        else:
            student[...] += product
    scores = student[...] / sharpness_divisor
    student[...] = scores
    top = jnp.max(scores, axis=1, keepdims=True)
    lse_s = top + jnp.log(jnp.sum(jnp.exp(scores - top), axis=1, keepdims=True))
    target = mentor[...].astype(f32) / sharpness_divisor
    cross = jnp.sum(prob[...] * (target - scores), axis=1, keepdims=True)
    lane = lax.broadcasted_iota(jnp.int32, (ROWS, 128), 1)
    columns = jnp.where(lane == 0, lse_s, jnp.where(lane == 1, lse_t[...], cross))
    flat = jnp.transpose(columns)
    lines = [flat[i : i + 1, h * 128 : (h + 1) * 128] for i in range(3) for h in range(2)]
    chunk = jnp.concatenate(lines, axis=0)
    stats[...] = jnp.broadcast_to(chunk[None], stats.shape)


def halves_kernel(core, a, b, c, d0, d1, own, mine, theirs):
    pieces = [(0, a, 0, 4), (1, b, 0, 4), (3, c, 0, 4), (2, d0, 0, 2), (2, d1, 2, 2)]
    for offset, ref, first, count in pieces:
        for i in range(count):
            j = first + i
            slab = 4 * (j % 2) + lax.rem(own[0] + offset - 2 * j + 8, 4)
            rows = pl.ds(pl.multiple_of(slab * SLAB, SLAB), SLAB)

            @pl.when(core[0] == j // 2)
            def _(ref=ref, rows=rows, i=i):
                mine[rows] = ref[pl.ds(i * SLAB, SLAB)]

            @pl.when(core[0] != j // 2)
            def _(ref=ref, rows=rows, i=i):
                theirs[rows] = ref[pl.ds(i * SLAB, SLAB)]


def lse_of_shards(parts):
    top = jnp.max(parts, axis=0)
    return top + jnp.log(jnp.sum(jnp.exp(parts - top[None]), axis=0))


def as_column(lines):
    flat = jnp.concatenate([lines[0:1], lines[1:2]], axis=1)
    return jnp.transpose(jnp.broadcast_to(flat, (128, ROWS)))[:, 0:1]


def times_head(held, sems, fetch, score, outs):
    for k, ref in outs:
        fetch(k).wait()
        ref[...] = lax.dot_general(
            held[k], score, (((1,), (1,)), ((), ())), preferred_element_type=f32
        ).astype(ref.dtype)


def fetcher(own, head, held, sems, places):
    def fetch(k):
        offset, j = places[k]
        rows = pl.ds(slab_row(own[0], offset, j), SLAB)
        return pltpu.make_async_copy(head.at[rows], held.at[k], sems.at[k])

    return fetch


def score_kernel(own, student, mentor, stats, head, score, b, c, mismatch, held, sems):
    places = [(1, j) for j in range(4)] + [(3, j) for j in range(4)]
    fetch = fetcher(own, head, held, sems, places)
    for k in range(8):
        fetch(k).start()
    parts = stats[...]
    all_s, all_t = lse_of_shards(parts[:, 0:2]), lse_of_shards(parts[:, 2:4])
    cross = jnp.sum(jnp.exp(parts[:, 2:4] - all_t[None]) * parts[:, 4:6], axis=0)
    mismatch[...] = sharpness_divisor * sharpness_divisor * (cross + all_s - all_t)
    target = mentor[...].astype(f32) / sharpness_divisor
    gap = jnp.exp(student[...] - as_column(all_s)) - jnp.exp(target - as_column(all_t))
    rounded = (objective_factor * sharpness_divisor * gap).astype(bf16)
    score[...] = rounded
    outs = [(k, (b, c)[k // 4].at[pl.ds((k % 4) * SLAB, SLAB)]) for k in range(8)]
    times_head(held, sems, fetch, rounded, outs)


def rest_kernel(own, score, head, d0, d1, a, held, sems):
    places = [(2, j) for j in range(4)] + [(0, j) for j in range(4)]
    fetch = fetcher(own, head, held, sems, places)
    for k in range(8):
        fetch(k).start()
    outs = [(k, (d0, d1)[k // 2].at[pl.ds((k % 2) * SLAB, SLAB)]) for k in range(4)]
    outs += [(4 + j, a.at[pl.ds(j * SLAB, SLAB)]) for j in range(4)]
    times_head(held, sems, fetch, score[...], outs)


def weight_kernel(mine, theirs, score, score_theirs, out):
    total = jnp.dot(mine[...], score[...], preferred_element_type=f32)
    total += jnp.dot(theirs[...], score_theirs[...], preferred_element_type=f32)
    out[...] = total.astype(out.dtype)


def weight_grad_of(mine, theirs, score, score_theirs):
    tile = 256
    rows = pl.BlockSpec((tile, ROWS), lambda i: (i, 0))
    whole = pl.BlockSpec((ROWS, COLS), lambda i: (0, 0))
    return pl.pallas_call(
        weight_kernel,
        grid=(FULL // 2 // tile,),
        out_shape=jax.ShapeDtypeStruct((FULL // 2, COLS), bf16),
        in_specs=[rows, rows, whole, whole],
        out_specs=pl.BlockSpec((tile, COLS), lambda i: (i, 0)),
        compiler_params=pltpu.CompilerParams(vmem_limit_bytes=16 * MIB),
        cost_estimate=pl.CostEstimate(flops=2 * FULL * ROWS * COLS, bytes_accessed=7 * MIB, transcendentals=0),
    )(mine, theirs, score, score_theirs)


def shards(hidden, head_weight, mentor_outputs):
    here = lax.axis_index("vocab")
    core = lax.axis_index("rows").astype(jnp.int32)[None]
    own = lax.rem(here // NZ % NX + 2 * (here // (NZ * NX)), 4).astype(jnp.int32)[None]

    a = trade(jnp.broadcast_to(hidden.T[None], (32, 32, ROWS)), class_groups).reshape(1024, ROWS)
    prob, lse_t = call(
        target_kernel,
        [((ROWS, COLS), f32), ((ROWS, 128), f32)],
        [("v", mentor_outputs)],
        10 * ROWS * COLS,
        2 * MIB,
    )
    b, c = step(a, 0, -1), step(a, 0, 1)
    d0, d1 = step(a[:512], 1, 0), step(a[512:], -1, 0)

    slots = [pltpu.VMEM((16, SLAB, COLS), bf16), pltpu.SemaphoreType.DMA((16,))]
    student, stats = call(
        student_kernel,
        [((ROWS, COLS), f32), ((128, 6, 128), f32)],
        [("s", own), ("v", a), ("v", b), ("v", c), ("v", d0), ("v", d1), ("h", head_weight)]
        + [("v", mentor_outputs), ("v", prob), ("v", lse_t)],
        2 * FULL * ROWS * COLS,
        12 * MIB,
        slots,
    )
    stats = trade(stats, None)
    mine, theirs = call(
        halves_kernel,
        [((FULL // 2, ROWS), bf16)] * 2,
        [("s", core), ("v", a), ("v", b), ("v", c), ("v", d0), ("v", d1), ("s", own)],
        0,
        4 * MIB,
    )
    theirs = other_core(theirs)

    slots = [pltpu.VMEM((8, SLAB, COLS), bf16), pltpu.SemaphoreType.DMA((8,))]
    score, b, c, mismatch = call(
        score_kernel,
        [((ROWS, COLS), bf16), ((1024, ROWS), bf16), ((1024, ROWS), bf16), ((2, 128), f32)],
        [("s", own), ("v", student), ("v", mentor_outputs), ("v", stats), ("h", head_weight)],
        FULL * ROWS * COLS,
        8 * MIB,
        slots,
    )
    b, c = step(b, 0, 1), step(c, 0, -1)
    score_theirs = other_core(score)
    d0, d1, a = call(
        rest_kernel,
        [((512, ROWS), bf16), ((512, ROWS), bf16), ((1024, ROWS), f32)],
        [("s", own), ("v", score), ("h", head_weight)],
        FULL * ROWS * COLS,
        7 * MIB,
        slots,
    )
    d0, d1 = step(d0, 1, 0), step(d1, -1, 0)
    weight_grad = weight_grad_of(mine, theirs, score, score_theirs)
    part = a + b.astype(f32) + c.astype(f32) + jnp.concatenate([d0, d1], axis=0).astype(f32)
    part = trade(part.astype(bf16).reshape(32, 32, ROWS), class_groups)
    hidden_grad = jnp.sum(part.astype(f32), axis=0).astype(bf16).T
    return (hidden_grad, weight_grad, mismatch.reshape(ROWS))


def solution(mesh):
    return jax.shard_map(
        shards,
        mesh=mesh,
        in_specs=(P("rows", "vocab"), P(None, "vocab"), P("rows", "vocab")),
        out_specs=(P("rows", "vocab"), P("rows", "vocab"), P("rows")),
        check_vma=False,
    )
```

```python
import jax
import jax.numpy as jnp
from jax import lax
from jax.experimental import pallas as pl
from jax.experimental.pallas import tpu as pltpu
from jax.sharding import PartitionSpec as P

sharpness_divisor = 2.0
objective_factor = 32.0

NY, NX, NZ = 4, 4, 8
ROWS, FULL, COLS, SLAB = 256, 4096, 1024, 256
f32, bf16 = jnp.float32, jnp.bfloat16
MIB = 1 << 20


def place(y, x, z):
    return ((y % NY) * NX + x % NX) * NZ + z % NZ


class_groups = [
    [place(y, c - 2 * y, z) for y in range(NY) for z in range(NZ)] for c in range(4)
]


def trade(chunks, groups):
    return lax.all_to_all(chunks, "vocab", 0, 0, tiled=True, axis_index_groups=groups)


def step(value, dy, dx):
    pairs = [
        (place(y, x, z), place(y + dy, x + dx, z))
        for y in range(NY)
        for x in range(NX)
        for z in range(NZ)
    ]
    return lax.ppermute(value, "vocab", pairs)


def other_core(value):
    return lax.ppermute(value, "rows", [(0, 1), (1, 0)])


def slab_row(own, offset, j):
    slab = 4 * j + lax.rem(own + offset - 2 * j + 8, 4)
    return pl.multiple_of(slab * SLAB, SLAB)


def call(body, outs, ins, flops, traffic, scratch=(), limit=8):
    smem, vmem, hbm = pltpu.SMEM, pltpu.VMEM, pltpu.HBM
    spaces = {"s": smem, "v": vmem, "h": hbm}
    return pl.pallas_call(
        body,
        out_shape=[jax.ShapeDtypeStruct(shape, dtype) for shape, dtype in outs],
        in_specs=[pl.BlockSpec(memory_space=spaces[kind]) for kind, _ in ins],
        out_specs=[pl.BlockSpec(memory_space=vmem) for _ in outs],
        scratch_shapes=list(scratch),
        compiler_params=pltpu.CompilerParams(vmem_limit_bytes=limit * MIB),
        cost_estimate=pl.CostEstimate(flops=flops, bytes_accessed=traffic, transcendentals=0),
    )(*[value for _, value in ins])


def target_kernel(mentor, head, prob, lse):
    target = mentor[...].astype(f32) / sharpness_divisor
    top = jnp.max(target, axis=1, keepdims=True)
    value = top + jnp.log(jnp.sum(jnp.exp(target - top), axis=1, keepdims=True))
    prob[...] = jnp.exp(target - value)
    lse[...] = jnp.broadcast_to(value, lse.shape)


def student_kernel(
    own, core, a, b, c, d0, d1, head, mentor, prob, lse_t, student, stats, mine, theirs
):
    for offset, ref, first, count in [(0, a, 0, 4), (1, b, 0, 4), (3, c, 0, 4), (2, d0, 0, 2), (2, d1, 2, 2)]:
        for i in range(count):
            j = first + i
            slab = 4 * (j % 2) + lax.rem(own[0] + offset - 2 * j + 8, 4)
            rows = pl.ds(pl.multiple_of(slab * SLAB, SLAB), SLAB)

            @pl.when(core[0] == j // 2)
            def _(ref=ref, rows=rows, i=i):
                mine[rows] = ref[pl.ds(i * SLAB, SLAB)]

            @pl.when(core[0] != j // 2)
            def _(ref=ref, rows=rows, i=i):
                theirs[rows] = ref[pl.ds(i * SLAB, SLAB)]

    half = FULL // 2

    def product(part, which):
        rows = pl.ds(pl.multiple_of(which * half, half), half)
        return lax.dot_general(
            part[...], head[rows], (((0,), (0,)), ((), ())), preferred_element_type=f32
        )

    scores = (product(mine, core[0]) + product(theirs, 1 - core[0])) / sharpness_divisor
    student[...] = scores
    top = jnp.max(scores, axis=1, keepdims=True)
    lse_s = top + jnp.log(jnp.sum(jnp.exp(scores - top), axis=1, keepdims=True))
    target = mentor[...].astype(f32) / sharpness_divisor
    cross = jnp.sum(prob[...] * (target - scores), axis=1, keepdims=True)
    lane = lax.broadcasted_iota(jnp.int32, (ROWS, 128), 1)
    columns = jnp.where(lane == 0, lse_s, jnp.where(lane == 1, lse_t[...], cross))
    flat = jnp.transpose(columns)
    lines = [flat[i : i + 1, h * 128 : (h + 1) * 128] for i in range(3) for h in range(2)]
    chunk = jnp.concatenate(lines, axis=0)
    stats[...] = jnp.broadcast_to(chunk[None], stats.shape)


def as_column(lines):
    flat = jnp.concatenate([lines[0:1], lines[1:2]], axis=1)
    return jnp.transpose(jnp.broadcast_to(flat, (128, ROWS)))[:, 0:1]


def times_head(own, head, score_t, outs):
    for offset, j, ref in outs:
        rows = pl.ds(slab_row(own[0], offset, j), SLAB)
        ref[...] = jnp.dot(head[rows], score_t, preferred_element_type=f32).astype(ref.dtype)


def score_kernel(own, student, mentor, stats, head, score, score_t, b, c, mismatch):
    parts = stats[...]
    top = jnp.max(parts, axis=0)
    weight = jnp.exp(parts - top[None])
    total = jnp.sum(weight, axis=0)
    lse = top + jnp.log(total)
    all_s, all_t = lse[0:2], lse[2:4]
    cross = jnp.sum(weight[:, 2:4] * parts[:, 4:6], axis=0) / total[2:4]
    mismatch[...] = sharpness_divisor * sharpness_divisor * (cross + all_s - all_t)
    target = mentor[...].astype(f32) / sharpness_divisor
    gap = jnp.exp(student[...] - as_column(all_s)) - jnp.exp(target - as_column(all_t))
    rounded = (objective_factor * sharpness_divisor * gap).astype(bf16)
    score[...] = rounded
    score_t[...] = jnp.transpose(rounded)
    outs = [(o, j, r.at[pl.ds(j * SLAB, SLAB)]) for o, r in ((1, b), (3, c)) for j in range(4)]
    times_head(own, head, score_t[...], outs)


def rest_kernel(own, score_t, head, d0, d1, a):
    outs = [(2, j, (d0, d1)[j // 2].at[pl.ds((j % 2) * SLAB, SLAB)]) for j in range(4)]
    outs += [(0, j, a.at[pl.ds(j * SLAB, SLAB)]) for j in range(4)]
    times_head(own, head, score_t[...], outs)


def weight_kernel(mine, theirs, score, score_theirs, out):
    total = jnp.dot(mine[...], score[...], preferred_element_type=f32)
    total += jnp.dot(theirs[...], score_theirs[...], preferred_element_type=f32)
    out[...] = total.astype(out.dtype)


def weight_grad_of(mine, theirs, score, score_theirs):
    tile = 256
    rows = pl.BlockSpec((tile, ROWS), lambda i: (i, 0))
    whole = pl.BlockSpec((ROWS, COLS), lambda i: (0, 0))
    return pl.pallas_call(
        weight_kernel,
        grid=(FULL // 2 // tile,),
        out_shape=jax.ShapeDtypeStruct((FULL // 2, COLS), bf16),
        in_specs=[rows, rows, whole, whole],
        out_specs=pl.BlockSpec((tile, COLS), lambda i: (i, 0)),
        compiler_params=pltpu.CompilerParams(vmem_limit_bytes=8 * MIB),
        cost_estimate=pl.CostEstimate(flops=2 * FULL * ROWS * COLS, bytes_accessed=7 * MIB, transcendentals=0),
    )(mine, theirs, score, score_theirs)


def shards(hidden, head_weight, mentor_outputs):
    here = lax.axis_index("vocab")
    core = lax.axis_index("rows").astype(jnp.int32)[None]
    own = lax.rem(here // NZ % NX + 2 * (here // (NZ * NX)), 4).astype(jnp.int32)[None]

    a = trade(jnp.broadcast_to(hidden.T[None], (32, 32, ROWS)), class_groups).reshape(1024, ROWS)
    prob, lse_t = call(
        target_kernel,
        [((ROWS, COLS), f32), ((ROWS, 128), f32)],
        [("v", mentor_outputs), ("v", head_weight)],
        10 * ROWS * COLS,
        2 * MIB,
    )
    b, c = step(a, 0, -1), step(a, 0, 1)
    d0, d1 = step(a[:512], 1, 0), step(a[512:], -1, 0)

    student, stats, mine, theirs = call(
        student_kernel,
        [((ROWS, COLS), f32), ((128, 6, 128), f32)] + [((FULL // 2, ROWS), bf16)] * 2,
        [("s", own), ("s", core), ("v", a), ("v", b), ("v", c), ("v", d0), ("v", d1), ("v", head_weight)]
        + [("v", mentor_outputs), ("v", prob), ("v", lse_t)],
        2 * FULL * ROWS * COLS,
        12 * MIB,
    )
    stats, theirs = lax.optimization_barrier((trade(stats, None), theirs))
    theirs = other_core(theirs)

    score, score_t, b, c, mismatch = call(
        score_kernel,
        [((ROWS, COLS), bf16), ((COLS, ROWS), bf16)] + [((1024, ROWS), bf16)] * 2 + [((2, 128), f32)],
        [("s", own), ("v", student), ("v", mentor_outputs), ("v", stats), ("v", head_weight)],
        FULL * ROWS * COLS,
        8 * MIB,
    )
    b, c = step(b, 0, 1), step(c, 0, -1)
    score_theirs = other_core(score)
    d0, d1, a = call(
        rest_kernel,
        [((512, ROWS), bf16), ((512, ROWS), bf16), ((1024, ROWS), f32)],
        [("s", own), ("v", score_t), ("v", head_weight)],
        FULL * ROWS * COLS,
        7 * MIB,
    )
    d0, d1 = step(d0, 1, 0), step(d1, -1, 0)
    weight_grad = weight_grad_of(mine, theirs, score, score_theirs)
    b, c, d0, d1, weight_grad = lax.optimization_barrier((b, c, d0, d1, weight_grad))
    part = a + b.astype(f32) + c.astype(f32) + jnp.concatenate([d0, d1], axis=0).astype(f32)
    part = trade(part.astype(bf16).reshape(32, 32, ROWS), class_groups)
    hidden_grad = jnp.sum(part.astype(f32), axis=0).astype(bf16).T
    return (hidden_grad, weight_grad, mismatch.reshape(ROWS))


def solution(mesh):
    return jax.shard_map(
        shards,
        mesh=mesh,
        in_specs=(P("rows", "vocab"), P(None, "vocab"), P("rows", "vocab")),
        out_specs=(P("rows", "vocab"), P("rows", "vocab"), P("rows")),
        check_vma=False,
    )
```

```python
import jax
import jax.numpy as jnp
from jax import lax
from jax.experimental import pallas as pl
from jax.experimental.pallas import tpu as pltpu
from jax.sharding import PartitionSpec as P

sharpness_divisor = 2.0
objective_factor = 32.0

NY, NX, NZ = 4, 4, 8
ROWS, FULL, COLS, SLAB = 256, 4096, 1024, 256
f32, bf16 = jnp.float32, jnp.bfloat16
MIB = 1 << 20


def place(y, x, z):
    return ((y % NY) * NX + x % NX) * NZ + z % NZ


class_groups = [
    [place(y, c - 2 * y, z) for y in range(NY) for z in range(NZ)] for c in range(4)
]


def trade(chunks, groups):
    return lax.all_to_all(chunks, "vocab", 0, 0, tiled=True, axis_index_groups=groups)


def step(value, dy, dx):
    pairs = [
        (place(y, x, z), place(y + dy, x + dx, z))
        for y in range(NY)
        for x in range(NX)
        for z in range(NZ)
    ]
    return lax.ppermute(value, "vocab", pairs)


def other_core(value):
    return lax.ppermute(value, "rows", [(0, 1), (1, 0)])


def slab_row(own, offset, j):
    slab = 4 * j + lax.rem(own + offset - 2 * j + 8, 4)
    return pl.multiple_of(slab * SLAB, SLAB)


def call(body, outs, ins, flops, traffic, scratch=(), limit=8, into="v"):
    smem, vmem, hbm = pltpu.SMEM, pltpu.VMEM, pltpu.HBM
    spaces = {"s": smem, "v": vmem, "h": hbm}
    return pl.pallas_call(
        body,
        out_shape=[jax.ShapeDtypeStruct(shape, dtype) for shape, dtype in outs],
        in_specs=[pl.BlockSpec(memory_space=spaces[kind]) for kind, _ in ins],
        out_specs=[pl.BlockSpec(memory_space=spaces[into]) for _ in outs],
        scratch_shapes=list(scratch),
        compiler_params=pltpu.CompilerParams(vmem_limit_bytes=limit * MIB),
        cost_estimate=pl.CostEstimate(flops=flops, bytes_accessed=traffic, transcendentals=0),
    )(*[value for _, value in ins])


def target_kernel(mentor, head, prob, lse):
    target = mentor[...].astype(f32) / sharpness_divisor
    top = jnp.max(target, axis=1, keepdims=True)
    value = top + jnp.log(jnp.sum(jnp.exp(target - top), axis=1, keepdims=True))
    prob[...] = jnp.exp(target - value)
    lse[...] = jnp.broadcast_to(value, lse.shape)


def student_kernel(
    own, core, a, b, c, d0, d1, head, mentor, prob, lse_t, rise, peak, stats, mine, theirs
):
    for offset, ref, first, count in [(0, a, 0, 4), (1, b, 0, 4), (3, c, 0, 4), (2, d0, 0, 2), (2, d1, 2, 2)]:
        for i in range(count):
            j = first + i
            slab = 4 * (j % 2) + lax.rem(own[0] + offset - 2 * j + 8, 4)
            rows = pl.ds(pl.multiple_of(slab * SLAB, SLAB), SLAB)

            @pl.when(core[0] == j // 2)
            def _(ref=ref, rows=rows, i=i):
                mine[rows] = ref[pl.ds(i * SLAB, SLAB)]

            @pl.when(core[0] != j // 2)
            def _(ref=ref, rows=rows, i=i):
                theirs[rows] = ref[pl.ds(i * SLAB, SLAB)]

    half = FULL // 2

    def product(part, which):
        rows = pl.ds(pl.multiple_of(which * half, half), half)
        return lax.dot_general(
            part[...], head[rows], (((0,), (0,)), ((), ())), preferred_element_type=f32
        )

    scores = (product(mine, core[0]) + product(theirs, 1 - core[0])) / sharpness_divisor
    top = jnp.max(scores, axis=1, keepdims=True)
    grown = jnp.exp(scores - top)
    rise[...] = grown
    peak[...] = jnp.broadcast_to(top, peak.shape)
    lse_s = top + jnp.log(jnp.sum(grown, axis=1, keepdims=True))
    target = mentor[...].astype(f32) / sharpness_divisor
    cross = jnp.sum(prob[...] * (target - scores), axis=1, keepdims=True)
    lane = lax.broadcasted_iota(jnp.int32, (ROWS, 128), 1)
    columns = jnp.where(lane == 0, lse_s, jnp.where(lane == 1, lse_t[...], cross))
    flat = jnp.transpose(columns)
    lines = [flat[i : i + 1, h * 128 : (h + 1) * 128] for i in range(3) for h in range(2)]
    stats[...] = jnp.concatenate(lines + lines[:2], axis=0)


def as_columns(first, second):
    lines = [jnp.concatenate([v[0:1], v[1:2]], axis=1) for v in (first, second)]
    flat = jnp.transpose(jnp.concatenate(lines * 4, axis=0))
    return flat[:, 0:1], flat[:, 1:2]


def merged(parts):
    top = jnp.max(parts, axis=0)
    weight = jnp.exp(parts - top[None])
    total = jnp.sum(weight, axis=0)
    lse = top + jnp.log(total)
    cross = jnp.sum(weight[:, 2:4] * parts[:, 4:6], axis=0) / total[2:4]
    return lse[0:2], lse[2:4], cross


def merge_kernel(first, second, third, fourth, stats):
    all_s, all_t, cross = merged(jnp.stack([r[...] for r in (first, second, third, fourth)]))
    chunk = jnp.concatenate([all_s, all_t, cross, cross], axis=0)
    stats[...] = jnp.broadcast_to(chunk[None], stats.shape)


def times_head(own, head, score_t, outs):
    for offset, j, ref in outs:
        rows = pl.ds(slab_row(own[0], offset, j), SLAB)
        ref[...] = jnp.dot(head[rows], score_t, preferred_element_type=f32).astype(ref.dtype)


def score_kernel(own, rise, peak, prob, lse_t, stats, head, score, score_t, b, c, mismatch):
    all_s, all_t, cross = merged(stats[...])
    mismatch[...] = sharpness_divisor * sharpness_divisor * (cross + all_s - all_t)
    end_s, end_t = as_columns(all_s, all_t)
    scale = objective_factor * sharpness_divisor
    share_s = scale * jnp.exp(peak[:, 0:1] - end_s)
    share_t = scale * jnp.exp(lse_t[:, 0:1] - end_t)
    rounded = (rise[...] * share_s - prob[...] * share_t).astype(bf16)
    score[...] = rounded
    score_t[...] = jnp.transpose(rounded)
    outs = [(o, j, r.at[pl.ds(j * SLAB, SLAB)]) for o, r in ((1, b), (3, c)) for j in range(4)]
    times_head(own, head, score_t[...], outs)


def rest_kernel(own, score_t, head, d0, d1, a):
    outs = [(2, j, (d0, d1)[j // 2].at[pl.ds((j % 2) * SLAB, SLAB)]) for j in range(4)]
    outs += [(0, j, a.at[pl.ds(j * SLAB, SLAB)]) for j in range(4)]
    times_head(own, head, score_t[...], outs)


def weight_kernel(mine, theirs, score, score_theirs, out, held, sems):
    def send(i):
        return pltpu.make_async_copy(held.at[i], out.at[pl.ds(i * SLAB, SLAB)], sems.at[i])

    for i in range(8):
        rows = pl.ds(i * SLAB, SLAB)
        total = jnp.dot(mine[rows], score[...], preferred_element_type=f32)
        total += jnp.dot(theirs[rows], score_theirs[...], preferred_element_type=f32)
        held[i] = total.astype(bf16)
        send(i).start()
    for i in range(8):
        send(i).wait()


def stats_of_all(stats):
    near = [stats, step(stats, 0, 1), step(stats, 0, -1), step(stats, 1, 0)]
    (stats,) = call(
        merge_kernel, [((32, 8, 128), f32)], [("v", value) for value in near], 1000, 1000
    )
    return trade(stats, class_groups)


def shards(hidden, head_weight, mentor_outputs):
    here = lax.axis_index("vocab")
    core = lax.axis_index("rows").astype(jnp.int32)[None]
    own = lax.rem(here // NZ % NX + 2 * (here // (NZ * NX)), 4).astype(jnp.int32)[None]

    a = trade(jnp.broadcast_to(hidden.T[None], (32, 32, ROWS)), class_groups).reshape(1024, ROWS)
    prob, lse_t = call(
        target_kernel,
        [((ROWS, COLS), f32), ((ROWS, 128), f32)],
        [("v", mentor_outputs), ("v", head_weight)],
        10 * ROWS * COLS,
        2 * MIB,
    )
    b, c = step(a, 0, -1), step(a, 0, 1)
    d0, d1 = step(a[:512], 1, 0), step(a[512:], -1, 0)

    rise, peak, stats, mine, theirs = call(
        student_kernel,
        [((ROWS, COLS), f32), ((ROWS, 128), f32), ((8, 128), f32)] + [((FULL // 2, ROWS), bf16)] * 2,
        [("s", own), ("s", core), ("v", a), ("v", b), ("v", c), ("v", d0), ("v", d1), ("v", head_weight)]
        + [("v", mentor_outputs), ("v", prob), ("v", lse_t)],
        2 * FULL * ROWS * COLS,
        12 * MIB,
    )
    stats, theirs = lax.optimization_barrier((stats_of_all(stats), theirs))
    theirs = other_core(theirs)

    score, score_t, b, c, mismatch = call(
        score_kernel,
        [((ROWS, COLS), bf16), ((COLS, ROWS), bf16)] + [((1024, ROWS), bf16)] * 2 + [((2, 128), f32)],
        [("s", own), ("v", rise), ("v", peak), ("v", prob), ("v", lse_t), ("v", stats), ("v", head_weight)],
        FULL * ROWS * COLS,
        8 * MIB,
    )
    b, c = step(b, 0, 1), step(c, 0, -1)
    score_theirs = other_core(score)
    d0, d1, a = call(
        rest_kernel,
        [((512, ROWS), bf16), ((512, ROWS), bf16), ((1024, ROWS), f32)],
        [("s", own), ("v", score_t), ("v", head_weight)],
        FULL * ROWS * COLS,
        7 * MIB,
    )
    d0, d1 = step(d0, 1, 0), step(d1, -1, 0)
    (weight_grad,) = call(
        weight_kernel,
        [((FULL // 2, COLS), bf16)],
        [("v", mine), ("v", theirs), ("v", score), ("v", score_theirs)],
        2 * FULL * ROWS * COLS,
        7 * MIB,
        [pltpu.VMEM((8, SLAB, COLS), bf16), pltpu.SemaphoreType.DMA((8,))],
        into="h",
    )
    b, c, d0, d1, weight_grad = lax.optimization_barrier((b, c, d0, d1, weight_grad))
    part = a + b.astype(f32) + c.astype(f32) + jnp.concatenate([d0, d1], axis=0).astype(f32)
    part = trade(part.astype(bf16).reshape(32, 32, ROWS), class_groups)
    hidden_grad = jnp.sum(part.astype(f32), axis=0).astype(bf16).T
    return (hidden_grad, weight_grad, mismatch.reshape(ROWS))


def solution(mesh):
    return jax.shard_map(
        shards,
        mesh=mesh,
        in_specs=(P("rows", "vocab"), P(None, "vocab"), P("rows", "vocab")),
        out_specs=(P("rows", "vocab"), P("rows", "vocab"), P("rows")),
        check_vma=False,
    )
```

```python
import jax
import jax.numpy as jnp
from jax import lax
from jax.experimental import pallas as pl
from jax.experimental.pallas import tpu as pltpu
from jax.sharding import PartitionSpec as P

sharpness_divisor = 2.0
objective_factor = 32.0

NY, NX, NZ = 4, 4, 8
ROWS, FULL, COLS, SLAB = 256, 4096, 1024, 256
f32, bf16 = jnp.float32, jnp.bfloat16
MIB = 1 << 20


def place(y, x, z):
    return ((y % NY) * NX + x % NX) * NZ + z % NZ


BOTH = ("vocab", "rows")


def spot(along, across, z, core):
    return place(*((across, along) if core == 0 else (along, across)), z) * 2 + core


class_groups = [
    [spot((c - 2 * across) % 4, across, z, core) for across in range(4) for z in range(NZ)]
    for core in range(2)
    for c in range(4)
]


def trade(chunks):
    return lax.all_to_all(chunks, BOTH, 0, 0, tiled=True, axis_index_groups=class_groups)


def step(value, across_by, along_by):
    pairs = [
        (spot(along, across, z, core), spot(along + along_by, across + across_by, z, core))
        for along in range(4)
        for across in range(4)
        for z in range(NZ)
        for core in range(2)
    ]
    return lax.ppermute(value, BOTH, pairs)


def other_core(value):
    return lax.ppermute(value, "rows", [(0, 1), (1, 0)])


def slab_of(own, core, offset, j):
    k = lax.rem(own[0] + offset - 2 * j + 8, 4)
    return (4 - 3 * core[0]) * j + (1 + 3 * core[0]) * k


def slab_row(own, core, offset, j):
    return pl.multiple_of(slab_of(own, core, offset, j) * SLAB, SLAB)


def call(body, outs, ins, flops, traffic, scratch=(), limit=8, into="v"):
    smem, vmem, hbm = pltpu.SMEM, pltpu.VMEM, pltpu.HBM
    spaces = {"s": smem, "v": vmem, "h": hbm}
    return pl.pallas_call(
        body,
        out_shape=[jax.ShapeDtypeStruct(shape, dtype) for shape, dtype in outs],
        in_specs=[pl.BlockSpec(memory_space=spaces[kind]) for kind, _ in ins],
        out_specs=[pl.BlockSpec(memory_space=spaces[into]) for _ in outs],
        scratch_shapes=list(scratch),
        compiler_params=pltpu.CompilerParams(vmem_limit_bytes=limit * MIB),
        cost_estimate=pl.CostEstimate(flops=flops, bytes_accessed=traffic, transcendentals=0),
    )(*[value for _, value in ins])


def target_kernel(mentor, head, prob, lse):
    target = mentor[...].astype(f32) / sharpness_divisor
    top = jnp.max(target, axis=1, keepdims=True)
    value = top + jnp.log(jnp.sum(jnp.exp(target - top), axis=1, keepdims=True))
    prob[...] = jnp.exp(target - value)
    lse[...] = jnp.broadcast_to(value, lse.shape)


def student_kernel(
    own, core, a, b, c, d0, d1, head, mentor, prob, lse_t, rise, peak, stats, mine, theirs
):
    for offset, ref, first, count in [(0, a, 0, 4), (1, b, 0, 4), (3, c, 0, 4), (2, d0, 0, 2), (2, d1, 2, 2)]:
        for i in range(count):
            slab = slab_of(own, core, offset, first + i)
            half = lax.shift_right_logical(slab, 3)
            rows = pl.ds(pl.multiple_of((slab - 8 * half) * SLAB, SLAB), SLAB)

            @pl.when(core[0] == half)
            def _(ref=ref, rows=rows, i=i):
                mine[rows] = ref[pl.ds(i * SLAB, SLAB)]

            @pl.when(core[0] != half)
            def _(ref=ref, rows=rows, i=i):
                theirs[rows] = ref[pl.ds(i * SLAB, SLAB)]

    half = FULL // 2

    def product(part, which):
        rows = pl.ds(pl.multiple_of(which * half, half), half)
        return lax.dot_general(
            part[...], head[rows], (((0,), (0,)), ((), ())), preferred_element_type=f32
        )

    scores = (product(mine, core[0]) + product(theirs, 1 - core[0])) / sharpness_divisor
    top = jnp.max(scores, axis=1, keepdims=True)
    grown = jnp.exp(scores - top)
    rise[...] = grown
    peak[...] = jnp.broadcast_to(top, peak.shape)
    lse_s = top + jnp.log(jnp.sum(grown, axis=1, keepdims=True))
    target = mentor[...].astype(f32) / sharpness_divisor
    cross = jnp.sum(prob[...] * (target - scores), axis=1, keepdims=True)
    lane = lax.broadcasted_iota(jnp.int32, (ROWS, 128), 1)
    columns = jnp.where(lane == 0, lse_s, jnp.where(lane == 1, lse_t[...], cross))
    flat = jnp.transpose(columns)
    lines = [flat[i : i + 1, h * 128 : (h + 1) * 128] for i in range(3) for h in range(2)]
    stats[...] = jnp.concatenate(lines, axis=0)


def as_columns(first, second):
    lines = [jnp.concatenate([v[0:1], v[1:2]], axis=1) for v in (first, second)]
    flat = jnp.transpose(jnp.concatenate(lines * 4, axis=0))
    return flat[:, 0:1], flat[:, 1:2]


def merged(parts):
    top = jnp.max(parts, axis=0)
    weight = jnp.exp(parts - top[None])
    total = jnp.sum(weight, axis=0)
    lse = top + jnp.log(total)
    cross = jnp.sum(weight[:, 2:4] * parts[:, 4:6], axis=0) / total[2:4]
    return lse[0:2], lse[2:4], cross


def merge_kernel(first, second, third, fourth, stats):
    all_s, all_t, cross = merged(jnp.stack([r[...] for r in (first, second, third, fourth)]))
    chunk = jnp.concatenate([all_s, all_t, cross], axis=0)
    stats[...] = jnp.broadcast_to(chunk[None], stats.shape)


def times_head(own, core, head, score_t, outs):
    for offset, j, ref in outs:
        rows = pl.ds(slab_row(own, core, offset, j), SLAB)
        ref[...] = jnp.dot(head[rows], score_t, preferred_element_type=f32).astype(ref.dtype)


def score_kernel(own, core, rise, peak, prob, lse_t, stats, head, score, score_t, b, c, mismatch):
    all_s, all_t, cross = merged(stats[...])
    mismatch[...] = sharpness_divisor * sharpness_divisor * (cross + all_s - all_t)
    end_s, end_t = as_columns(all_s, all_t)
    scale = objective_factor * sharpness_divisor
    share_s = scale * jnp.exp(peak[:, 0:1] - end_s)
    share_t = scale * jnp.exp(lse_t[:, 0:1] - end_t)
    rounded = (rise[...] * share_s - prob[...] * share_t).astype(bf16)
    score[...] = rounded
    score_t[...] = jnp.transpose(rounded)
    outs = [(o, j, r.at[pl.ds(j * SLAB, SLAB)]) for o, r in ((1, b), (3, c)) for j in range(4)]
    times_head(own, core, head, score_t[...], outs)


def rest_kernel(own, core, score_t, head, d0, d1, a):
    outs = [(2, j, (d0, d1)[j // 2].at[pl.ds((j % 2) * SLAB, SLAB)]) for j in range(4)]
    outs += [(0, j, a.at[pl.ds(j * SLAB, SLAB)]) for j in range(4)]
    times_head(own, core, head, score_t[...], outs)


def weight_kernel(mine, theirs, score, score_theirs, out, held, sems):
    def send(i):
        return pltpu.make_async_copy(held.at[i], out.at[pl.ds(i * SLAB, SLAB)], sems.at[i])

    for i in range(8):
        rows = pl.ds(i * SLAB, SLAB)
        total = jnp.dot(mine[rows], score[...], preferred_element_type=f32)
        total += jnp.dot(theirs[rows], score_theirs[...], preferred_element_type=f32)
        held[i] = total.astype(bf16)
        send(i).start()
    for i in range(8):
        send(i).wait()


def stats_of_all(stats):
    near = [stats, step(stats, 0, 1), step(stats, 0, -1), step(stats, 1, 0)]
    (stats,) = call(
        merge_kernel, [((32, 6, 128), f32)], [("v", value) for value in near], 1000, 1000
    )
    return trade(stats)


def shards(hidden, head_weight, mentor_outputs):
    here = lax.axis_index("vocab")
    core = lax.axis_index("rows").astype(jnp.int32)
    x, y = lax.rem(lax.div(here, NZ), NX), lax.div(here, NZ * NX)
    own = lax.rem(jnp.where(core == 0, x + 2 * y, y + 2 * x), 4).astype(jnp.int32)[None]
    core = core[None]

    a = trade(jnp.broadcast_to(hidden.T[None], (32, 32, ROWS))).reshape(1024, ROWS)
    prob, lse_t = call(
        target_kernel,
        [((ROWS, COLS), f32), ((ROWS, 128), f32)],
        [("v", mentor_outputs), ("v", head_weight)],
        10 * ROWS * COLS,
        2 * MIB,
    )
    b, c = step(a, 0, -1), step(a, 0, 1)
    d0, d1 = step(a[:512], 1, 0), step(a[512:], -1, 0)

    rise, peak, stats, mine, theirs = call(
        student_kernel,
        [((ROWS, COLS), f32), ((ROWS, 128), f32), ((6, 128), f32)] + [((FULL // 2, ROWS), bf16)] * 2,
        [("s", own), ("s", core), ("v", a), ("v", b), ("v", c), ("v", d0), ("v", d1), ("v", head_weight)]
        + [("v", mentor_outputs), ("v", prob), ("v", lse_t)],
        2 * FULL * ROWS * COLS,
        12 * MIB,
    )
    stats, theirs = lax.optimization_barrier((stats_of_all(stats), theirs))
    theirs = other_core(theirs)

    score, score_t, b, c, mismatch = call(
        score_kernel,
        [((ROWS, COLS), bf16), ((COLS, ROWS), bf16)] + [((1024, ROWS), bf16)] * 2 + [((2, 128), f32)],
        [("s", own), ("s", core), ("v", rise), ("v", peak), ("v", prob), ("v", lse_t), ("v", stats), ("v", head_weight)],
        FULL * ROWS * COLS,
        8 * MIB,
    )
    b, c = step(b, 0, 1), step(c, 0, -1)
    score_theirs = other_core(score)
    d0, d1, a = call(
        rest_kernel,
        [((512, ROWS), bf16), ((512, ROWS), bf16), ((1024, ROWS), f32)],
        [("s", own), ("s", core), ("v", score_t), ("v", head_weight)],
        FULL * ROWS * COLS,
        7 * MIB,
    )
    d0, d1 = step(d0, 1, 0), step(d1, -1, 0)
    (weight_grad,) = call(
        weight_kernel,
        [((FULL // 2, COLS), bf16)],
        [("v", mine), ("v", theirs), ("v", score), ("v", score_theirs)],
        2 * FULL * ROWS * COLS,
        7 * MIB,
        [pltpu.VMEM((8, SLAB, COLS), bf16), pltpu.SemaphoreType.DMA((8,))],
        into="h",
    )
    b, c, d0, d1, weight_grad = lax.optimization_barrier((b, c, d0, d1, weight_grad))
    part = a + b.astype(f32) + c.astype(f32) + jnp.concatenate([d0, d1], axis=0).astype(f32)
    part = trade(part.astype(bf16).reshape(32, 32, ROWS))
    hidden_grad = jnp.sum(part.astype(f32), axis=0).astype(bf16).T
    return (hidden_grad, weight_grad, mismatch.reshape(ROWS))


def solution(mesh):
    return jax.shard_map(
        shards,
        mesh=mesh,
        in_specs=(P("rows", "vocab"), P(None, "vocab"), P("rows", "vocab")),
        out_specs=(P("rows", "vocab"), P("rows", "vocab"), P("rows")),
        check_vma=False,
    )
```

```python
import jax
import jax.numpy as jnp
from jax import lax
from jax.experimental import pallas as pl
from jax.experimental.pallas import tpu as pltpu
from jax.sharding import PartitionSpec as P

sharpness_divisor = 2.0
objective_factor = 32.0

NY, NX, NZ = 4, 4, 8
ROWS, FULL, COLS, SLAB = 256, 4096, 1024, 256
f32, bf16 = jnp.float32, jnp.bfloat16
MIB = 1 << 20


def place(y, x, z):
    return ((y % NY) * NX + x % NX) * NZ + z % NZ


BOTH = ("vocab", "rows")


def spot(along, across, z, core):
    return place(*((across, along) if core == 0 else (along, across)), z) * 2 + core


class_groups = [
    [spot((c - 2 * across) % 4, across, z, core) for across in range(4) for z in range(NZ)]
    for core in range(2)
    for c in range(4)
]


z_groups = [[place(y, x, z) for z in range(NZ)] for y in range(NY) for x in range(NX)]


def trade(chunks):
    return lax.all_to_all(chunks, BOTH, 0, 0, tiled=True, axis_index_groups=class_groups)


def class_of(hidden_t):
    slab = lax.all_to_all(
        jnp.broadcast_to(hidden_t[None], (NZ, 32, ROWS)), "vocab", 0, 0, tiled=True, axis_index_groups=z_groups
    ).reshape(SLAB, ROWS)
    return jnp.concatenate([slab] + [step(slab, i, -2 * i) for i in (1, 2, 3)], axis=0)


def step(value, across_by, along_by):
    pairs = [
        (spot(along, across, z, core), spot(along + along_by, across + across_by, z, core))
        for along in range(4)
        for across in range(4)
        for z in range(NZ)
        for core in range(2)
    ]
    return lax.ppermute(value, BOTH, pairs)


def other_core(value):
    return lax.ppermute(value, "rows", [(0, 1), (1, 0)])


def slab_of(own, core, offset, j):
    k = lax.rem(own[0] + offset - 2 * j + 8, 4)
    return (4 - 3 * core[0]) * j + (1 + 3 * core[0]) * k


def slab_row(own, core, offset, j):
    return pl.multiple_of(slab_of(own, core, offset, j) * SLAB, SLAB)


def call(body, outs, ins, flops, traffic, scratch=(), limit=8, into="v"):
    smem, vmem, hbm = pltpu.SMEM, pltpu.VMEM, pltpu.HBM
    spaces = {"s": smem, "v": vmem, "h": hbm}
    return pl.pallas_call(
        body,
        out_shape=[jax.ShapeDtypeStruct(shape, dtype) for shape, dtype in outs],
        in_specs=[pl.BlockSpec(memory_space=spaces[kind]) for kind, _ in ins],
        out_specs=[pl.BlockSpec(memory_space=spaces[into]) for _ in outs],
        scratch_shapes=list(scratch),
        compiler_params=pltpu.CompilerParams(vmem_limit_bytes=limit * MIB),
        cost_estimate=pl.CostEstimate(flops=flops, bytes_accessed=traffic, transcendentals=0),
    )(*[value for _, value in ins])


def target_kernel(mentor, head, prob, lse):
    target = mentor[...].astype(f32) / sharpness_divisor
    top = jnp.max(target, axis=1, keepdims=True)
    value = top + jnp.log(jnp.sum(jnp.exp(target - top), axis=1, keepdims=True))
    prob[...] = jnp.exp(target - value)
    lse[...] = jnp.broadcast_to(value, lse.shape)


def student_kernel(
    own, core, column, a, b, c, d0, d1, head, mentor, prob, lse_t, rise, peak, stats, mine, theirs
):
    for offset, ref, shift, count in [(0, a, 0, 4), (1, b, 0, 4), (3, c, 0, 4), (2, d0, -1, 2), (2, d1, 1, 2)]:
        for i in range(count):
            j = lax.rem(column[0] + shift - i + 4, 4)
            slab = slab_of(own, core, offset, j)
            half = lax.shift_right_logical(slab, 3)
            rows = pl.ds(pl.multiple_of((slab - 8 * half) * SLAB, SLAB), SLAB)

            @pl.when(core[0] == half)
            def _(ref=ref, rows=rows, i=i):
                mine[rows] = ref[pl.ds(i * SLAB, SLAB)]

            @pl.when(core[0] != half)
            def _(ref=ref, rows=rows, i=i):
                theirs[rows] = ref[pl.ds(i * SLAB, SLAB)]

    half = FULL // 2

    def product(part, which):
        rows = pl.ds(pl.multiple_of(which * half, half), half)
        return lax.dot_general(
            part[...], head[rows], (((0,), (0,)), ((), ())), preferred_element_type=f32
        )

    scores = (product(mine, core[0]) + product(theirs, 1 - core[0])) / sharpness_divisor
    top = jnp.max(scores, axis=1, keepdims=True)
    grown = jnp.exp(scores - top)
    rise[...] = grown
    peak[...] = jnp.broadcast_to(top, peak.shape)
    lse_s = top + jnp.log(jnp.sum(grown, axis=1, keepdims=True))
    target = mentor[...].astype(f32) / sharpness_divisor
    cross = jnp.sum(prob[...] * (target - scores), axis=1, keepdims=True)
    lane = lax.broadcasted_iota(jnp.int32, (ROWS, 128), 1)
    columns = jnp.where(lane == 0, lse_s, jnp.where(lane == 1, lse_t[...], cross))
    flat = jnp.transpose(columns)
    lines = [flat[i : i + 1, h * 128 : (h + 1) * 128] for i in range(3) for h in range(2)]
    stats[...] = jnp.concatenate(lines, axis=0)


def as_columns(first, second):
    lines = [jnp.concatenate([v[0:1], v[1:2]], axis=1) for v in (first, second)]
    flat = jnp.transpose(jnp.concatenate(lines * 4, axis=0))
    return flat[:, 0:1], flat[:, 1:2]


def merged(parts):
    top = jnp.max(parts, axis=0)
    weight = jnp.exp(parts - top[None])
    total = jnp.sum(weight, axis=0)
    lse = top + jnp.log(total)
    cross = jnp.sum(weight[:, 2:4] * parts[:, 4:6], axis=0) / total[2:4]
    return lse[0:2], lse[2:4], cross


def merge_kernel(first, second, third, fourth, stats):
    all_s, all_t, cross = merged(jnp.stack([r[...] for r in (first, second, third, fourth)]))
    chunk = jnp.concatenate([all_s, all_t, cross], axis=0)
    stats[...] = jnp.broadcast_to(chunk[None], stats.shape)


def times_head(own, core, head, score_t, outs):
    for offset, j, ref in outs:
        rows = pl.ds(slab_row(own, core, offset, j), SLAB)
        ref[...] = jnp.dot(head[rows], score_t, preferred_element_type=f32).astype(ref.dtype)


def score_kernel(own, core, rise, peak, prob, lse_t, stats, head, score, score_t, b, c, mismatch):
    all_s, all_t, cross = merged(stats[...])
    mismatch[...] = sharpness_divisor * sharpness_divisor * (cross + all_s - all_t)
    end_s, end_t = as_columns(all_s, all_t)
    scale = objective_factor * sharpness_divisor
    share_s = scale * jnp.exp(peak[:, 0:1] - end_s)
    share_t = scale * jnp.exp(lse_t[:, 0:1] - end_t)
    rounded = (rise[...] * share_s - prob[...] * share_t).astype(bf16)
    score[...] = rounded
    score_t[...] = jnp.transpose(rounded)
    outs = [(o, j, r.at[pl.ds(j * SLAB, SLAB)]) for o, r in ((1, b), (3, c)) for j in range(4)]
    times_head(own, core, head, score_t[...], outs)


def rest_kernel(own, core, score_t, head, d0, d1, a):
    outs = [(2, j, (d0, d1)[j // 2].at[pl.ds((j % 2) * SLAB, SLAB)]) for j in range(4)]
    outs += [(0, j, a.at[pl.ds(j * SLAB, SLAB)]) for j in range(4)]
    times_head(own, core, head, score_t[...], outs)


def weight_kernel(mine, theirs, score, score_theirs, out, held, sems):
    def send(i):
        return pltpu.make_async_copy(held.at[i], out.at[pl.ds(i * SLAB, SLAB)], sems.at[i])

    for i in range(8):
        rows = pl.ds(i * SLAB, SLAB)
        total = jnp.dot(mine[rows], score[...], preferred_element_type=f32)
        total += jnp.dot(theirs[rows], score_theirs[...], preferred_element_type=f32)
        held[i] = total.astype(bf16)
        send(i).start()
    for i in range(8):
        send(i).wait()


def stats_of_all(stats):
    near = [stats, step(stats, 0, 1), step(stats, 0, -1), step(stats, 1, 0)]
    (stats,) = call(
        merge_kernel, [((32, 6, 128), f32)], [("v", value) for value in near], 1000, 1000
    )
    return trade(stats)


def shards(hidden, head_weight, mentor_outputs):
    here = lax.axis_index("vocab")
    core = lax.axis_index("rows").astype(jnp.int32)
    x, y = lax.rem(lax.div(here, NZ), NX), lax.div(here, NZ * NX)
    own = lax.rem(jnp.where(core == 0, x + 2 * y, y + 2 * x), 4).astype(jnp.int32)[None]
    core = core[None]

    column = jnp.where(core[0] == 0, y, x).astype(jnp.int32)[None]
    a = class_of(hidden.T)
    prob, lse_t = call(
        target_kernel,
        [((ROWS, COLS), f32), ((ROWS, 128), f32)],
        [("v", mentor_outputs), ("v", head_weight)],
        10 * ROWS * COLS,
        2 * MIB,
    )
    b, c = step(a, 0, -1), step(a, 0, 1)
    d0, d1 = step(a[:512], 1, 0), step(a[:512], -1, 0)

    rise, peak, stats, mine, theirs = call(
        student_kernel,
        [((ROWS, COLS), f32), ((ROWS, 128), f32), ((6, 128), f32)] + [((FULL // 2, ROWS), bf16)] * 2,
        [("s", own), ("s", core), ("s", column), ("v", a), ("v", b), ("v", c), ("v", d0), ("v", d1), ("v", head_weight)]
        + [("v", mentor_outputs), ("v", prob), ("v", lse_t)],
        2 * FULL * ROWS * COLS,
        12 * MIB,
    )
    stats, theirs = lax.optimization_barrier((stats_of_all(stats), theirs))
    theirs = other_core(theirs)

    score, score_t, b, c, mismatch = call(
        score_kernel,
        [((ROWS, COLS), bf16), ((COLS, ROWS), bf16)] + [((1024, ROWS), bf16)] * 2 + [((2, 128), f32)],
        [("s", own), ("s", core), ("v", rise), ("v", peak), ("v", prob), ("v", lse_t), ("v", stats), ("v", head_weight)],
        FULL * ROWS * COLS,
        8 * MIB,
    )
    b, c = step(b, 0, 1), step(c, 0, -1)
    score_theirs = other_core(score)
    d0, d1, a = call(
        rest_kernel,
        [((512, ROWS), bf16), ((512, ROWS), bf16), ((1024, ROWS), f32)],
        [("s", own), ("s", core), ("v", score_t), ("v", head_weight)],
        FULL * ROWS * COLS,
        7 * MIB,
    )
    d0, d1 = step(d0, 1, 0), step(d1, -1, 0)
    (weight_grad,) = call(
        weight_kernel,
        [((FULL // 2, COLS), bf16)],
        [("v", mine), ("v", theirs), ("v", score), ("v", score_theirs)],
        2 * FULL * ROWS * COLS,
        7 * MIB,
        [pltpu.VMEM((8, SLAB, COLS), bf16), pltpu.SemaphoreType.DMA((8,))],
        into="h",
    )
    b, c, d0, d1, weight_grad = lax.optimization_barrier((b, c, d0, d1, weight_grad))
    part = a + b.astype(f32) + c.astype(f32) + jnp.concatenate([d0, d1], axis=0).astype(f32)
    part = trade(part.astype(bf16).reshape(32, 32, ROWS))
    hidden_grad = jnp.sum(part.astype(f32), axis=0).astype(bf16).T
    return (hidden_grad, weight_grad, mismatch.reshape(ROWS))


def solution(mesh):
    return jax.shard_map(
        shards,
        mesh=mesh,
        in_specs=(P("rows", "vocab"), P(None, "vocab"), P("rows", "vocab")),
        out_specs=(P("rows", "vocab"), P("rows", "vocab"), P("rows")),
        check_vma=False,
    )
```

```python
import jax
import jax.numpy as jnp
from jax import lax
from jax.experimental import pallas as pl
from jax.experimental.pallas import tpu as pltpu
from jax.sharding import PartitionSpec as P

sharpness_divisor = 2.0
objective_factor = 32.0

NY, NX, NZ = 4, 4, 8
ROWS, FULL, COLS, SLAB = 256, 4096, 1024, 256
f32, bf16 = jnp.float32, jnp.bfloat16
MIB = 1 << 20


def place(y, x, z):
    return ((y % NY) * NX + x % NX) * NZ + z % NZ


BOTH = ("vocab", "rows")


def spot(along, across, z, core):
    return place(*((across, along) if core == 0 else (along, across)), z) * 2 + core


octets = [
    [spot(c + 2 * z, across, z, core) for z in range(NZ)]
    for core in range(2)
    for c in range(4)
    for across in range(4)
]
class_groups = [sum(octets[i : i + 4], []) for i in range(0, 32, 4)]


def trade(chunks, groups):
    return lax.all_to_all(chunks, BOTH, 0, 0, tiled=True, axis_index_groups=groups)


def step(value, along_by, across_by, z_by):
    pairs = [
        (spot(along, across, z, core), spot(along + along_by, across + across_by, z + z_by, core))
        for along in range(4)
        for across in range(4)
        for z in range(NZ)
        for core in range(2)
    ]
    return lax.ppermute(value, BOTH, pairs)


def class_of(hidden_t):
    slab = trade(jnp.broadcast_to(hidden_t[None], (NZ, 32, ROWS)), octets).reshape(SLAB, ROWS)
    return jnp.concatenate([slab] + [step(slab, 0, i, 0) for i in (1, 2, 3)], axis=0)


def other_core(value):
    return lax.ppermute(value, "rows", [(0, 1), (1, 0)])


def column_of(own, core, offset, j, odd):
    along = lax.rem(own[0] + offset + 2 * odd, 4)
    return (4 - 3 * core[0]) * j + (1 + 3 * core[0]) * along


def call(body, outs, ins, flops, traffic, scratch=(), limit=8, into="v"):
    smem, vmem, hbm = pltpu.SMEM, pltpu.VMEM, pltpu.HBM
    spaces = {"s": smem, "v": vmem, "h": hbm}
    return pl.pallas_call(
        body,
        out_shape=[jax.ShapeDtypeStruct(shape, dtype) for shape, dtype in outs],
        in_specs=[pl.BlockSpec(memory_space=spaces[kind]) for kind, _ in ins],
        out_specs=[pl.BlockSpec(memory_space=spaces[into]) for _ in outs],
        scratch_shapes=list(scratch),
        compiler_params=pltpu.CompilerParams(vmem_limit_bytes=limit * MIB),
        cost_estimate=pl.CostEstimate(flops=flops, bytes_accessed=traffic, transcendentals=0),
    )(*[value for _, value in ins])


def target_kernel(mentor, head, prob, lse):
    target = mentor[...].astype(f32) / sharpness_divisor
    top = jnp.max(target, axis=1, keepdims=True)
    value = top + jnp.log(jnp.sum(jnp.exp(target - top), axis=1, keepdims=True))
    prob[...] = jnp.exp(target - value)
    lse[...] = jnp.broadcast_to(value, lse.shape)


def student_kernel(
    own, core, column, a, b, c, d0, d1, head, mentor, prob, lse_t, rise, peak, stats, mine, theirs
):
    for offset, ref, first, count in [(0, a, 0, 4), (1, b, 0, 4), (3, c, 0, 4), (2, d0, 0, 2), (2, d1, 2, 2)]:
        for i in range(count):
            j = lax.rem(column[0] - first - i + 4, 4)
            for odd in range(2):
                place_in = column_of(own, core, offset, j, odd)
                half = lax.shift_right_logical(place_in, 3)
                base = (place_in - 8 * half) * SLAB

                def put(into, ref=ref, base=base, i=i, odd=odd):
                    for z in range(odd, NZ, 2):
                        rows = pl.ds(pl.multiple_of(base + 32 * z, 32), 32)
                        into[rows] = ref[pl.ds(i * SLAB + 32 * z, 32)]

                @pl.when(core[0] == half)
                def _(put=put):
                    put(mine)

                @pl.when(core[0] != half)
                def _(put=put):
                    put(theirs)

    half = FULL // 2

    def product(part, which):
        rows = pl.ds(pl.multiple_of(which * half, half), half)
        return lax.dot_general(
            part[...], head[rows], (((0,), (0,)), ((), ())), preferred_element_type=f32
        )

    scores = (product(mine, core[0]) + product(theirs, 1 - core[0])) / sharpness_divisor
    top = jnp.max(scores, axis=1, keepdims=True)
    grown = jnp.exp(scores - top)
    rise[...] = grown
    peak[...] = jnp.broadcast_to(top, peak.shape)
    lse_s = top + jnp.log(jnp.sum(grown, axis=1, keepdims=True))
    target = mentor[...].astype(f32) / sharpness_divisor
    cross = jnp.sum(prob[...] * (target - scores), axis=1, keepdims=True)
    lane = lax.broadcasted_iota(jnp.int32, (ROWS, 128), 1)
    columns = jnp.where(lane == 0, lse_s, jnp.where(lane == 1, lse_t[...], cross))
    flat = jnp.transpose(columns)
    lines = [flat[i : i + 1, h * 128 : (h + 1) * 128] for i in range(3) for h in range(2)]
    stats[...] = jnp.concatenate(lines, axis=0)


def as_columns(first, second):
    lines = [jnp.concatenate([v[0:1], v[1:2]], axis=1) for v in (first, second)]
    flat = jnp.transpose(jnp.concatenate(lines * 4, axis=0))
    return flat[:, 0:1], flat[:, 1:2]


def merged(parts):
    top = jnp.max(parts, axis=0)
    weight = jnp.exp(parts - top[None])
    total = jnp.sum(weight, axis=0)
    lse = top + jnp.log(total)
    cross = jnp.sum(weight[:, 2:4] * parts[:, 4:6], axis=0) / total[2:4]
    return lse[0:2], lse[2:4], cross


def merge_kernel(first, second, third, fourth, stats):
    all_s, all_t, cross = merged(jnp.stack([r[...] for r in (first, second, third, fourth)]))
    chunk = jnp.concatenate([all_s, all_t, cross], axis=0)
    stats[...] = jnp.broadcast_to(chunk[None], stats.shape)


def times_head(own, core, head, score_t, outs):
    for offset, j, ref in outs:
        bases = [column_of(own, core, offset, j, odd) * SLAB for odd in range(2)]
        eighths = [head[pl.ds(pl.multiple_of(bases[z % 2] + 32 * z, 32), 32)] for z in range(NZ)]
        rows = jnp.concatenate(eighths, axis=0)
        ref[...] = jnp.dot(rows, score_t, preferred_element_type=f32).astype(ref.dtype)


def score_kernel(own, core, rise, peak, prob, lse_t, stats, head, score, score_t, b, c, mismatch):
    all_s, all_t, cross = merged(stats[...])
    mismatch[...] = sharpness_divisor * sharpness_divisor * (cross + all_s - all_t)
    end_s, end_t = as_columns(all_s, all_t)
    scale = objective_factor * sharpness_divisor
    share_s = scale * jnp.exp(peak[:, 0:1] - end_s)
    share_t = scale * jnp.exp(lse_t[:, 0:1] - end_t)
    rounded = (rise[...] * share_s - prob[...] * share_t).astype(bf16)
    score[...] = rounded
    score_t[...] = jnp.transpose(rounded)
    outs = [(o, j, r.at[pl.ds(j * SLAB, SLAB)]) for o, r in ((1, b), (3, c)) for j in range(4)]
    times_head(own, core, head, score_t[...], outs)


def rest_kernel(own, core, score_t, head, d0, d1, a):
    outs = [(2, j, (d0, d1)[j // 2].at[pl.ds((j % 2) * SLAB, SLAB)]) for j in range(4)]
    outs += [(0, j, a.at[pl.ds(j * SLAB, SLAB)]) for j in range(4)]
    times_head(own, core, head, score_t[...], outs)


def weight_kernel(mine, theirs, score, score_theirs, out, held, sems):
    def send(i):
        return pltpu.make_async_copy(held.at[i], out.at[pl.ds(i * SLAB, SLAB)], sems.at[i])

    for i in range(8):
        rows = pl.ds(i * SLAB, SLAB)
        total = jnp.dot(mine[rows], score[...], preferred_element_type=f32)
        total += jnp.dot(theirs[rows], score_theirs[...], preferred_element_type=f32)
        held[i] = total.astype(bf16)
        send(i).start()
    for i in range(8):
        send(i).wait()


def stats_of_all(stats):
    near = [stats, step(stats, 1, 0, 0), step(stats, -1, 0, 0), step(stats, 0, 0, 1)]
    (stats,) = call(
        merge_kernel, [((32, 6, 128), f32)], [("v", value) for value in near], 1000, 1000
    )
    return trade(stats, class_groups)


def shards(hidden, head_weight, mentor_outputs):
    here = lax.axis_index("vocab")
    core = lax.axis_index("rows").astype(jnp.int32)
    x, y = lax.rem(lax.div(here, NZ), NX), lax.div(here, NZ * NX)
    own = lax.rem(jnp.where(core == 0, x, y) + 2 * lax.rem(here, NZ), 4).astype(jnp.int32)[None]
    core = core[None]

    column = jnp.where(core[0] == 0, y, x).astype(jnp.int32)[None]
    a = class_of(hidden.T)
    prob, lse_t = call(
        target_kernel,
        [((ROWS, COLS), f32), ((ROWS, 128), f32)],
        [("v", mentor_outputs), ("v", head_weight)],
        10 * ROWS * COLS,
        2 * MIB,
    )
    b, c = step(a, -1, 0, 0), step(a, 1, 0, 0)
    d0, d1 = step(a[:512], 0, 0, 1), step(a[512:], 0, 0, -1)

    rise, peak, stats, mine, theirs = call(
        student_kernel,
        [((ROWS, COLS), f32), ((ROWS, 128), f32), ((6, 128), f32)] + [((FULL // 2, ROWS), bf16)] * 2,
        [("s", own), ("s", core), ("s", column), ("v", a), ("v", b), ("v", c), ("v", d0), ("v", d1), ("v", head_weight)]
        + [("v", mentor_outputs), ("v", prob), ("v", lse_t)],
        2 * FULL * ROWS * COLS,
        12 * MIB,
    )
    stats, theirs = lax.optimization_barrier((stats_of_all(stats), theirs))
    theirs = other_core(theirs)

    score, score_t, b, c, mismatch = call(
        score_kernel,
        [((ROWS, COLS), bf16), ((COLS, ROWS), bf16)] + [((1024, ROWS), bf16)] * 2 + [((2, 128), f32)],
        [("s", own), ("s", core), ("v", rise), ("v", peak), ("v", prob), ("v", lse_t), ("v", stats), ("v", head_weight)],
        FULL * ROWS * COLS,
        8 * MIB,
    )
    b, c = step(b, 1, 0, 0), step(c, -1, 0, 0)
    score_theirs = other_core(score)
    d0, d1, a = call(
        rest_kernel,
        [((512, ROWS), bf16), ((512, ROWS), bf16), ((1024, ROWS), f32)],
        [("s", own), ("s", core), ("v", score_t), ("v", head_weight)],
        FULL * ROWS * COLS,
        7 * MIB,
    )
    d0, d1 = step(d0, 0, 0, 1), step(d1, 0, 0, -1)
    (weight_grad,) = call(
        weight_kernel,
        [((FULL // 2, COLS), bf16)],
        [("v", mine), ("v", theirs), ("v", score), ("v", score_theirs)],
        2 * FULL * ROWS * COLS,
        7 * MIB,
        [pltpu.VMEM((8, SLAB, COLS), bf16), pltpu.SemaphoreType.DMA((8,))],
        into="h",
    )
    b, c, d0, d1, weight_grad = lax.optimization_barrier((b, c, d0, d1, weight_grad))
    part = a + b.astype(f32) + c.astype(f32) + jnp.concatenate([d0, d1], axis=0).astype(f32)
    part = trade(part.astype(bf16).reshape(32, 32, ROWS), class_groups)
    hidden_grad = jnp.sum(part.astype(f32), axis=0).astype(bf16).T
    return (hidden_grad, weight_grad, mismatch.reshape(ROWS))


def solution(mesh):
    return jax.shard_map(
        shards,
        mesh=mesh,
        in_specs=(P("rows", "vocab"), P(None, "vocab"), P("rows", "vocab")),
        out_specs=(P("rows", "vocab"), P("rows", "vocab"), P("rows")),
        check_vma=False,
    )
```

```python
import jax
import jax.numpy as jnp
from jax import lax
from jax.experimental import pallas as pl
from jax.experimental.pallas import tpu as pltpu
from jax.sharding import PartitionSpec as P

sharpness_divisor = 2.0
objective_factor = 32.0

NY, NX, NZ = 4, 4, 8
ROWS, FULL, COLS, SLAB = 256, 4096, 1024, 256
f32, bf16 = jnp.float32, jnp.bfloat16
MIB = 1 << 20


def place(y, x, z):
    return ((y % NY) * NX + x % NX) * NZ + z % NZ


BOTH = ("vocab", "rows")


def spot(along, across, z, core):
    return place(*((across, along) if core == 0 else (along, across)), z) * 2 + core


octets = [
    [spot(c + 2 * z, across, z, core) for z in range(NZ)]
    for core in range(2)
    for c in range(4)
    for across in range(4)
]
class_groups = [sum(octets[i : i + 4], []) for i in range(0, 32, 4)]


def trade(chunks, groups):
    return lax.all_to_all(chunks, BOTH, 0, 0, tiled=True, axis_index_groups=groups)


def step(value, along_by, across_by, z_by):
    pairs = [
        (spot(along, across, z, core), spot(along + along_by, across + across_by, z + z_by, core))
        for along in range(4)
        for across in range(4)
        for z in range(NZ)
        for core in range(2)
    ]
    return lax.ppermute(value, BOTH, pairs)


def class_of(hidden_t):
    slab = trade(jnp.broadcast_to(hidden_t[None], (NZ, 32, ROWS)), octets).reshape(SLAB, ROWS)
    return jnp.concatenate([slab] + [step(slab, 0, i, 0) for i in (1, 2, 3)], axis=0)


def other_core(value):
    return lax.ppermute(value, "rows", [(0, 1), (1, 0)])


def column_of(own, core, offset, j, odd):
    along = lax.rem(own[0] + offset + 2 * odd, 4)
    return (4 - 3 * core[0]) * j + (1 + 3 * core[0]) * along


def call(body, outs, ins, flops, traffic, scratch=(), limit=8, into="v"):
    smem, vmem, hbm = pltpu.SMEM, pltpu.VMEM, pltpu.HBM
    spaces = {"s": smem, "v": vmem, "h": hbm}
    return pl.pallas_call(
        body,
        out_shape=[jax.ShapeDtypeStruct(shape, dtype) for shape, dtype in outs],
        in_specs=[pl.BlockSpec(memory_space=spaces[kind]) for kind, _ in ins],
        out_specs=[pl.BlockSpec(memory_space=spaces[into]) for _ in outs],
        scratch_shapes=list(scratch),
        compiler_params=pltpu.CompilerParams(vmem_limit_bytes=limit * MIB),
        cost_estimate=pl.CostEstimate(flops=flops, bytes_accessed=traffic, transcendentals=0),
    )(*[value for _, value in ins])


def target_kernel(mentor, head, prob, lse):
    target = mentor[...].astype(f32) / sharpness_divisor
    top = jnp.max(target, axis=1, keepdims=True)
    value = top + jnp.log(jnp.sum(jnp.exp(target - top), axis=1, keepdims=True))
    prob[...] = jnp.exp(target - value)
    lse[...] = jnp.broadcast_to(value, lse.shape)


def student_kernel(
    own, core, column, a, b, c, d0, d1, head, mentor, prob, lse_t, rise, peak, stats, mine, theirs
):
    for offset, ref, first, count in [(0, a, 0, 4), (1, b, 0, 4), (3, c, 0, 4), (2, d0, 0, 2), (2, d1, 2, 2)]:
        for i in range(count):
            j = lax.rem(column[0] - first - i + 4, 4)
            for odd in range(2):
                place_in = column_of(own, core, offset, j, odd)
                half = lax.shift_right_logical(place_in, 3)
                base = (place_in - 8 * half) * SLAB

                def put(into, ref=ref, base=base, i=i, odd=odd):
                    for z in range(odd, NZ, 2):
                        rows = pl.ds(pl.multiple_of(base + 32 * z, 32), 32)
                        into[rows] = ref[pl.ds(i * SLAB + 32 * z, 32)]

                @pl.when(core[0] == half)
                def _(put=put):
                    put(mine)

                @pl.when(core[0] != half)
                def _(put=put):
                    put(theirs)

    half = FULL // 2

    def product(part, which):
        rows = pl.ds(pl.multiple_of(which * half, half), half)
        return lax.dot_general(
            part[...], head[rows], (((0,), (0,)), ((), ())), preferred_element_type=f32
        )

    scores = (product(mine, core[0]) + product(theirs, 1 - core[0])) / sharpness_divisor
    top = jnp.max(scores, axis=1, keepdims=True)
    grown = jnp.exp(scores - top)
    rise[...] = grown
    peak[...] = jnp.broadcast_to(top, peak.shape)
    lse_s = top + jnp.log(jnp.sum(grown, axis=1, keepdims=True))
    target = mentor[...].astype(f32) / sharpness_divisor
    cross = jnp.sum(prob[...] * (target - scores), axis=1, keepdims=True)
    lane = lax.broadcasted_iota(jnp.int32, (ROWS, 128), 1)
    columns = jnp.where(lane == 0, lse_s, jnp.where(lane == 1, lse_t[...], cross))
    flat = jnp.transpose(columns)
    lines = [flat[i : i + 1, h * 128 : (h + 1) * 128] for i in range(3) for h in range(2)]
    stats[...] = jnp.concatenate(lines, axis=0)


def as_columns(first, second):
    lines = [jnp.concatenate([v[0:1], v[1:2]], axis=1) for v in (first, second)]
    flat = jnp.transpose(jnp.concatenate(lines * 4, axis=0))
    return flat[:, 0:1], flat[:, 1:2]


def merged(parts):
    top = jnp.max(parts, axis=0)
    weight = jnp.exp(parts - top[None])
    total = jnp.sum(weight, axis=0)
    lse = top + jnp.log(total)
    cross = jnp.sum(weight[:, 2:4] * parts[:, 4:6], axis=0) / total[2:4]
    return lse[0:2], lse[2:4], cross


def merge_kernel(first, second, third, fourth, stats):
    all_s, all_t, cross = merged(jnp.stack([r[...] for r in (first, second, third, fourth)]))
    chunk = jnp.concatenate([all_s, all_t, cross], axis=0)
    stats[...] = jnp.broadcast_to(chunk[None], stats.shape)


def times_head(own, core, column, head, score_t, outs):
    for offset, back, ref in outs:
        j = lax.rem(column[0] - back + 4, 4)
        bases = [column_of(own, core, offset, j, odd) * SLAB for odd in range(2)]
        eighths = [head[pl.ds(pl.multiple_of(bases[z % 2] + 32 * z, 32), 32)] for z in range(NZ)]
        rows = jnp.concatenate(eighths, axis=0)
        ref[...] = jnp.dot(rows, score_t, preferred_element_type=f32).astype(ref.dtype)


def score_kernel(own, core, column, rise, peak, prob, lse_t, stats, head, score, score_t, b, c, mismatch):
    all_s, all_t, cross = merged(stats[...])
    mismatch[...] = sharpness_divisor * sharpness_divisor * (cross + all_s - all_t)
    end_s, end_t = as_columns(all_s, all_t)
    scale = objective_factor * sharpness_divisor
    share_s = scale * jnp.exp(peak[:, 0:1] - end_s)
    share_t = scale * jnp.exp(lse_t[:, 0:1] - end_t)
    rounded = (rise[...] * share_s - prob[...] * share_t).astype(bf16)
    score[...] = rounded
    score_t[...] = jnp.transpose(rounded)
    outs = [(o, j, r.at[pl.ds(j * SLAB, SLAB)]) for o, r in ((1, b), (3, c)) for j in range(4)]
    times_head(own, core, column, head, score_t[...], outs)


def rest_kernel(own, core, column, score_t, head, d0, d1, a):
    outs = [(2, j, (d0, d1)[j // 2].at[pl.ds((j % 2) * SLAB, SLAB)]) for j in range(4)]
    outs += [(0, j, a.at[pl.ds(j * SLAB, SLAB)]) for j in range(4)]
    times_head(own, core, column, head, score_t[...], outs)


def weight_kernel(mine, theirs, score, score_theirs, out, held, sems):
    def send(i):
        return pltpu.make_async_copy(held.at[i], out.at[pl.ds(i * SLAB, SLAB)], sems.at[i])

    for i in range(8):
        rows = pl.ds(i * SLAB, SLAB)
        total = jnp.dot(mine[rows], score[...], preferred_element_type=f32)
        total += jnp.dot(theirs[rows], score_theirs[...], preferred_element_type=f32)
        held[i] = total.astype(bf16)
        send(i).start()
    for i in range(8):
        send(i).wait()


def stats_of_all(stats):
    near = [stats, step(stats, 1, 0, 0), step(stats, -1, 0, 0), step(stats, 0, 0, 1)]
    (stats,) = call(
        merge_kernel, [((32, 6, 128), f32)], [("v", value) for value in near], 1000, 1000
    )
    return trade(stats, class_groups)


def shards(hidden, head_weight, mentor_outputs):
    here = lax.axis_index("vocab")
    core = lax.axis_index("rows").astype(jnp.int32)
    x, y = lax.rem(lax.div(here, NZ), NX), lax.div(here, NZ * NX)
    own = lax.rem(jnp.where(core == 0, x, y) + 2 * lax.rem(here, NZ), 4).astype(jnp.int32)[None]
    core = core[None]

    column = jnp.where(core[0] == 0, y, x).astype(jnp.int32)[None]
    a = class_of(hidden.T)
    prob, lse_t = call(
        target_kernel,
        [((ROWS, COLS), f32), ((ROWS, 128), f32)],
        [("v", mentor_outputs), ("v", head_weight)],
        10 * ROWS * COLS,
        2 * MIB,
    )
    b, c = step(a, -1, 0, 0), step(a, 1, 0, 0)
    d0, d1 = step(a[:512], 0, 0, 1), step(a[512:], 0, 0, -1)

    rise, peak, stats, mine, theirs = call(
        student_kernel,
        [((ROWS, COLS), f32), ((ROWS, 128), f32), ((6, 128), f32)] + [((FULL // 2, ROWS), bf16)] * 2,
        [("s", own), ("s", core), ("s", column), ("v", a), ("v", b), ("v", c), ("v", d0), ("v", d1), ("v", head_weight)]
        + [("v", mentor_outputs), ("v", prob), ("v", lse_t)],
        2 * FULL * ROWS * COLS,
        12 * MIB,
    )
    stats, theirs = lax.optimization_barrier((stats_of_all(stats), theirs))
    theirs = other_core(theirs)

    score, score_t, b, c, mismatch = call(
        score_kernel,
        [((ROWS, COLS), bf16), ((COLS, ROWS), bf16)] + [((1024, ROWS), bf16)] * 2 + [((2, 128), f32)],
        [("s", own), ("s", core), ("s", column), ("v", rise), ("v", peak), ("v", prob), ("v", lse_t), ("v", stats), ("v", head_weight)],
        FULL * ROWS * COLS,
        8 * MIB,
    )
    b, c = step(b, 1, 0, 0), step(c, -1, 0, 0)
    score_theirs = other_core(score)
    d0, d1, a = call(
        rest_kernel,
        [((512, ROWS), bf16), ((512, ROWS), bf16), ((1024, ROWS), f32)],
        [("s", own), ("s", core), ("s", column), ("v", score_t), ("v", head_weight)],
        FULL * ROWS * COLS,
        7 * MIB,
    )
    d0, d1 = step(d0, 0, 0, 1), step(d1, 0, 0, -1)
    (weight_grad,) = call(
        weight_kernel,
        [((FULL // 2, COLS), bf16)],
        [("v", mine), ("v", theirs), ("v", score), ("v", score_theirs)],
        2 * FULL * ROWS * COLS,
        7 * MIB,
        [pltpu.VMEM((8, SLAB, COLS), bf16), pltpu.SemaphoreType.DMA((8,))],
        into="h",
    )
    b, c, d0, d1, weight_grad = lax.optimization_barrier((b, c, d0, d1, weight_grad))
    part = a + b.astype(f32) + c.astype(f32) + jnp.concatenate([d0, d1], axis=0).astype(f32)
    slabs = [part[i * SLAB : (i + 1) * SLAB] for i in range(4)]
    total = slabs[0]
    for i in (1, 2, 3):
        total += step(slabs[i].astype(bf16), 0, -i, 0).astype(f32)
    total = trade(total.astype(bf16).reshape(NZ, 32, ROWS), octets)
    hidden_grad = jnp.sum(total.astype(f32), axis=0).astype(bf16).T
    return (hidden_grad, weight_grad, mismatch.reshape(ROWS))


def solution(mesh):
    return jax.shard_map(
        shards,
        mesh=mesh,
        in_specs=(P("rows", "vocab"), P(None, "vocab"), P("rows", "vocab")),
        out_specs=(P("rows", "vocab"), P("rows", "vocab"), P("rows")),
        check_vma=False,
    )
```

```python
import jax
import jax.numpy as jnp
from jax import lax
from jax.experimental import pallas as pl
from jax.experimental.pallas import tpu as pltpu
from jax.sharding import PartitionSpec as P

sharpness_divisor = 2.0
objective_factor = 32.0

NY, NX, NZ = 4, 4, 8
ROWS, FULL, COLS, SLAB = 256, 4096, 1024, 256
f32, bf16 = jnp.float32, jnp.bfloat16
MIB = 1 << 20


def place(y, x, z):
    return ((y % NY) * NX + x % NX) * NZ + z % NZ


BOTH = ("vocab", "rows")


def spot(along, across, z, core):
    return place(*((across, along) if core == 0 else (along, across)), z) * 2 + core


octets = [
    [spot(c + 2 * z, across, z, core) for z in range(NZ)]
    for core in range(2)
    for c in range(4)
    for across in range(4)
]
class_groups = [sum(octets[i : i + 4], []) for i in range(0, 32, 4)]


def trade(chunks, groups):
    return lax.all_to_all(chunks, BOTH, 0, 0, tiled=True, axis_index_groups=groups)


def step(value, along_by, across_by, z_by):
    pairs = [
        (spot(along, across, z, core), spot(along + along_by, across + across_by, z + z_by, core))
        for along in range(4)
        for across in range(4)
        for z in range(NZ)
        for core in range(2)
    ]
    return lax.ppermute(value, BOTH, pairs)


def class_of(hidden_t):
    slab = trade(jnp.broadcast_to(hidden_t[None], (NZ, 32, ROWS)), octets).reshape(SLAB, ROWS)
    return jnp.concatenate([slab] + [step(slab, 0, i, 0) for i in (1, 2, 3)], axis=0)


def other_core(value):
    return lax.ppermute(value, "rows", [(0, 1), (1, 0)])


def column_of(own, core, offset, j, odd):
    along = lax.rem(own[0] + offset + 2 * odd, 4)
    return (4 - 3 * core[0]) * j + (1 + 3 * core[0]) * along


def call(body, outs, ins, flops, traffic, scratch=(), limit=8, into="v"):
    smem, vmem, hbm = pltpu.SMEM, pltpu.VMEM, pltpu.HBM
    spaces = {"s": smem, "v": vmem, "h": hbm}
    return pl.pallas_call(
        body,
        out_shape=[jax.ShapeDtypeStruct(shape, dtype) for shape, dtype in outs],
        in_specs=[pl.BlockSpec(memory_space=spaces[kind]) for kind, _ in ins],
        out_specs=[pl.BlockSpec(memory_space=spaces[into]) for _ in outs],
        scratch_shapes=list(scratch),
        compiler_params=pltpu.CompilerParams(vmem_limit_bytes=limit * MIB),
        cost_estimate=pl.CostEstimate(flops=flops, bytes_accessed=traffic, transcendentals=0),
    )(*[value for _, value in ins])


def target_kernel(mentor, head, prob, lse):
    target = mentor[...].astype(f32) / sharpness_divisor
    top = jnp.max(target, axis=1, keepdims=True)
    value = top + jnp.log(jnp.sum(jnp.exp(target - top), axis=1, keepdims=True))
    prob[...] = jnp.exp(target - value)
    lse[...] = jnp.broadcast_to(value, lse.shape)


def student_kernel(
    own, core, column, a, b, c, d0, d1, head, mentor, prob, lse_t, rise, peak, stats, mine, theirs
):
    for offset, ref, first, count in [(0, a, 0, 4), (1, b, 0, 4), (3, c, 0, 4), (2, d0, 0, 2), (2, d1, 2, 2)]:
        for i in range(count):
            j = lax.rem(column[0] - first - i + 4, 4)
            for odd in range(2):
                place_in = column_of(own, core, offset, j, odd)
                half = lax.shift_right_logical(place_in, 3)
                base = (place_in - 8 * half) * SLAB

                def put(into, ref=ref, base=base, i=i, odd=odd):
                    for z in range(odd, NZ, 2):
                        rows = pl.ds(pl.multiple_of(base + 32 * z, 32), 32)
                        into[rows] = ref[pl.ds(i * SLAB + 32 * z, 32)]

                @pl.when(core[0] == half)
                def _(put=put):
                    put(mine)

                @pl.when(core[0] != half)
                def _(put=put):
                    put(theirs)

    half = FULL // 2

    def product(part, which):
        rows = pl.ds(pl.multiple_of(which * half, half), half)
        return lax.dot_general(
            part[...], head[rows], (((0,), (0,)), ((), ())), preferred_element_type=f32
        )

    scores = (product(mine, core[0]) + product(theirs, 1 - core[0])) / sharpness_divisor
    top = jnp.max(scores, axis=1, keepdims=True)
    grown = jnp.exp(scores - top)
    rise[...] = grown
    peak[...] = jnp.broadcast_to(top, peak.shape)
    lse_s = top + jnp.log(jnp.sum(grown, axis=1, keepdims=True))
    target = mentor[...].astype(f32) / sharpness_divisor
    cross = jnp.sum(prob[...] * (target - scores), axis=1, keepdims=True)
    lane = lax.broadcasted_iota(jnp.int32, (ROWS, 128), 1)
    columns = jnp.where(lane == 0, lse_s, jnp.where(lane == 1, lse_t[...], cross))
    flat = jnp.transpose(columns)
    lines = [flat[i : i + 1, h * 128 : (h + 1) * 128] for i in range(3) for h in range(2)]
    stats[...] = jnp.concatenate(lines, axis=0)


def as_columns(first, second):
    lines = [jnp.concatenate([v[0:1], v[1:2]], axis=1) for v in (first, second)]
    flat = jnp.transpose(jnp.concatenate(lines * 4, axis=0))
    return flat[:, 0:1], flat[:, 1:2]


def merged(parts):
    top = jnp.max(parts, axis=0)
    weight = jnp.exp(parts - top[None])
    total = jnp.sum(weight, axis=0)
    lse = top + jnp.log(total)
    cross = jnp.sum(weight[:, 2:4] * parts[:, 4:6], axis=0) / total[2:4]
    return lse[0:2], lse[2:4], cross


def merge_kernel(first, second, third, fourth, stats):
    all_s, all_t, cross = merged(jnp.stack([r[...] for r in (first, second, third, fourth)]))
    chunk = jnp.concatenate([all_s, all_t, cross], axis=0)
    stats[...] = jnp.broadcast_to(chunk[None], stats.shape)


def times_head(own, core, column, head, score_t, outs):
    for offset, back, ref in outs:
        j = lax.rem(column[0] - back + 4, 4)
        bases = [column_of(own, core, offset, j, odd) * SLAB for odd in range(2)]
        eighths = [head[pl.ds(pl.multiple_of(bases[z % 2] + 32 * z, 32), 32)] for z in range(NZ)]
        rows = jnp.concatenate(eighths, axis=0)
        ref[...] = jnp.dot(rows, score_t, preferred_element_type=f32).astype(ref.dtype)


def score_kernel(own, core, column, rise, peak, prob, lse_t, stats, head, score, score_t, b, c, mismatch):
    all_s, all_t, cross = merged(stats[...])
    mismatch[...] = sharpness_divisor * sharpness_divisor * (cross + all_s - all_t)
    end_s, end_t = as_columns(all_s, all_t)
    scale = objective_factor * sharpness_divisor
    share_s = scale * jnp.exp(peak[:, 0:1] - end_s)
    share_t = scale * jnp.exp(lse_t[:, 0:1] - end_t)
    rounded = (rise[...] * share_s - prob[...] * share_t).astype(bf16)
    score[...] = rounded
    score_t[...] = jnp.transpose(rounded)
    outs = [(o, j, r.at[pl.ds(j * SLAB, SLAB)]) for o, r in ((1, b), (3, c)) for j in range(4)]
    times_head(own, core, column, head, score_t[...], outs)


def rest_kernel(own, core, column, score_t, head, d0, d1, a):
    outs = [(2, j, (d0, d1)[j // 2].at[pl.ds((j % 2) * SLAB, SLAB)]) for j in range(4)]
    outs += [(0, j, a.at[pl.ds(j * SLAB, SLAB)]) for j in range(4)]
    times_head(own, core, column, head, score_t[...], outs)


def weight_kernel(mine, theirs, score, score_theirs, out, held, sems):
    def send(i):
        return pltpu.make_async_copy(held.at[i], out.at[pl.ds(i * SLAB, SLAB)], sems.at[i])

    for i in range(8):
        rows = pl.ds(i * SLAB, SLAB)
        total = jnp.dot(mine[rows], score[...], preferred_element_type=f32)
        total += jnp.dot(theirs[rows], score_theirs[...], preferred_element_type=f32)
        held[i] = total.astype(bf16)
        send(i).start()
    for i in range(8):
        send(i).wait()


def stats_of_all(stats):
    near = [stats, step(stats, 1, 0, 0), step(stats, -1, 0, 0), step(stats, 0, 0, 1)]
    (stats,) = call(
        merge_kernel, [((32, 6, 128), f32)], [("v", value) for value in near], 1000, 1000
    )
    return trade(stats, class_groups)


def shards(hidden, head_weight, mentor_outputs):
    here = lax.axis_index("vocab")
    core = lax.axis_index("rows").astype(jnp.int32)
    x, y = lax.rem(lax.div(here, NZ), NX), lax.div(here, NZ * NX)
    own = lax.rem(jnp.where(core == 0, x, y) + 2 * lax.rem(here, NZ), 4).astype(jnp.int32)[None]
    core = core[None]

    column = jnp.where(core[0] == 0, y, x).astype(jnp.int32)[None]
    a = class_of(hidden.T)
    prob, lse_t = call(
        target_kernel,
        [((ROWS, COLS), f32), ((ROWS, 128), f32)],
        [("v", mentor_outputs), ("v", head_weight)],
        10 * ROWS * COLS,
        2 * MIB,
    )
    b, c = step(a, -1, 0, 0), step(a, 1, 0, 0)
    d0, d1 = step(a[:512], 0, 0, 1), step(a[512:], 0, 0, -1)

    rise, peak, stats, mine, theirs = call(
        student_kernel,
        [((ROWS, COLS), f32), ((ROWS, 128), f32), ((6, 128), f32)] + [((FULL // 2, ROWS), bf16)] * 2,
        [("s", own), ("s", core), ("s", column), ("v", a), ("v", b), ("v", c), ("v", d0), ("v", d1), ("v", head_weight)]
        + [("v", mentor_outputs), ("v", prob), ("v", lse_t)],
        2 * FULL * ROWS * COLS,
        12 * MIB,
    )
    stats = stats_of_all(stats)

    score, score_t, b, c, mismatch = call(
        score_kernel,
        [((ROWS, COLS), bf16), ((COLS, ROWS), bf16)] + [((1024, ROWS), bf16)] * 2 + [((2, 128), f32)],
        [("s", own), ("s", core), ("s", column), ("v", rise), ("v", peak), ("v", prob), ("v", lse_t), ("v", stats), ("v", head_weight)],
        FULL * ROWS * COLS,
        8 * MIB,
    )
    b, c = step(b, 1, 0, 0), step(c, -1, 0, 0)
    d0, d1, a = call(
        rest_kernel,
        [((512, ROWS), bf16), ((512, ROWS), bf16), ((1024, ROWS), f32)],
        [("s", own), ("s", core), ("s", column), ("v", score_t), ("v", head_weight)],
        FULL * ROWS * COLS,
        7 * MIB,
    )
    d0, d1 = step(d0, 0, 0, 1), step(d1, 0, 0, -1)
    part = a + b.astype(f32) + c.astype(f32) + jnp.concatenate([d0, d1], axis=0).astype(f32)
    part, theirs, score_theirs = lax.optimization_barrier((part, theirs, score))
    slabs = [part[i * SLAB : (i + 1) * SLAB] for i in range(4)]
    arrived = [step(slabs[i].astype(bf16), 0, -i, 0) for i in (1, 2, 3)]
    theirs, score_theirs = other_core(theirs), other_core(score_theirs)
    (weight_grad,) = call(
        weight_kernel,
        [((FULL // 2, COLS), bf16)],
        [("v", mine), ("v", theirs), ("v", score), ("v", score_theirs)],
        2 * FULL * ROWS * COLS,
        7 * MIB,
        [pltpu.VMEM((8, SLAB, COLS), bf16), pltpu.SemaphoreType.DMA((8,))],
        into="h",
    )
    *arrived, weight_grad = lax.optimization_barrier((*arrived, weight_grad))
    total = slabs[0]
    for value in arrived:
        total += value.astype(f32)
    total = trade(total.astype(bf16).reshape(NZ, 32, ROWS), octets)
    hidden_grad = jnp.sum(total.astype(f32), axis=0).astype(bf16).T
    return (hidden_grad, weight_grad, mismatch.reshape(ROWS))


def solution(mesh):
    return jax.shard_map(
        shards,
        mesh=mesh,
        in_specs=(P("rows", "vocab"), P(None, "vocab"), P("rows", "vocab")),
        out_specs=(P("rows", "vocab"), P("rows", "vocab"), P("rows")),
        check_vma=False,
    )
```

```python
import jax
import jax.numpy as jnp
from jax import lax
from jax.experimental import pallas as pl
from jax.experimental.pallas import tpu as pltpu
from jax.sharding import PartitionSpec as P

sharpness_divisor = 2.0
objective_factor = 32.0

NY, NX, NZ = 4, 4, 8
ROWS, FULL, COLS, SLAB = 256, 4096, 1024, 256
f32, bf16 = jnp.float32, jnp.bfloat16
MIB = 1 << 20


def place(y, x, z):
    return ((y % NY) * NX + x % NX) * NZ + z % NZ


BOTH = ("vocab", "rows")


def spot(along, across, z, core):
    return place(*((across, along) if core == 0 else (along, across)), z) * 2 + core


octets = [
    [spot(c + 2 * z, across, z, core) for z in range(NZ)]
    for core in range(2)
    for c in range(4)
    for across in range(4)
]
class_groups = [sum(octets[i : i + 4], []) for i in range(0, 32, 4)]


def trade(chunks, groups):
    return lax.all_to_all(chunks, BOTH, 0, 0, tiled=True, axis_index_groups=groups)


def step(value, along_by, across_by, z_by):
    pairs = [
        (spot(along, across, z, core), spot(along + along_by, across + across_by, z + z_by, core))
        for along in range(4)
        for across in range(4)
        for z in range(NZ)
        for core in range(2)
    ]
    return lax.ppermute(value, BOTH, pairs)


def class_of(hidden_t):
    slab = trade(jnp.broadcast_to(hidden_t[None], (NZ, 32, ROWS)), octets).reshape(SLAB, ROWS)
    return jnp.concatenate([slab] + [step(slab, 0, i, 0) for i in (1, 2, 3)], axis=0)


def other_core(value):
    return lax.ppermute(value, "rows", [(0, 1), (1, 0)])


def column_of(own, core, offset, j, odd):
    along = lax.rem(own[0] + offset + 2 * odd, 4)
    return (4 - 3 * core[0]) * j + (1 + 3 * core[0]) * along


def call(body, outs, ins, flops, traffic, scratch=(), limit=8, into="v"):
    smem, vmem, hbm = pltpu.SMEM, pltpu.VMEM, pltpu.HBM
    spaces = {"s": smem, "v": vmem, "h": hbm}
    return pl.pallas_call(
        body,
        out_shape=[jax.ShapeDtypeStruct(shape, dtype) for shape, dtype in outs],
        in_specs=[pl.BlockSpec(memory_space=spaces[kind]) for kind, _ in ins],
        out_specs=[pl.BlockSpec(memory_space=spaces[into]) for _ in outs],
        scratch_shapes=list(scratch),
        compiler_params=pltpu.CompilerParams(vmem_limit_bytes=limit * MIB),
        cost_estimate=pl.CostEstimate(flops=flops, bytes_accessed=traffic, transcendentals=0),
    )(*[value for _, value in ins])


def target_kernel(mentor, head, prob, lse):
    target = mentor[...].astype(f32) / sharpness_divisor
    top = jnp.max(target, axis=1, keepdims=True)
    value = top + jnp.log(jnp.sum(jnp.exp(target - top), axis=1, keepdims=True))
    prob[...] = jnp.exp(target - value)
    lse[...] = jnp.broadcast_to(value, lse.shape)


def student_kernel(
    own, core, column, a, b, c, d0, d1, head, mentor, prob, lse_t, rise, peak, stats, mine, theirs
):
    for offset, ref, first, count in [(0, a, 0, 4), (1, b, 0, 4), (3, c, 0, 4), (2, d0, 0, 2), (2, d1, 2, 2)]:
        for i in range(count):
            j = lax.rem(column[0] - first - i + 4, 4)
            for odd in range(2):
                place_in = column_of(own, core, offset, j, odd)
                half = lax.shift_right_logical(place_in, 3)
                base = (place_in - 8 * half) * SLAB

                def put(into, ref=ref, base=base, i=i, odd=odd):
                    for z in range(odd, NZ, 2):
                        rows = pl.ds(pl.multiple_of(base + 32 * z, 32), 32)
                        into[rows] = ref[pl.ds(i * SLAB + 32 * z, 32)]

                @pl.when(core[0] == half)
                def _(put=put):
                    put(mine)

                @pl.when(core[0] != half)
                def _(put=put):
                    put(theirs)

    half = FULL // 2

    def product(part, which):
        rows = pl.ds(pl.multiple_of(which * half, half), half)
        return lax.dot_general(
            part[...], head[rows], (((0,), (0,)), ((), ())), preferred_element_type=f32
        )

    scores = (product(mine, core[0]) + product(theirs, 1 - core[0])) / sharpness_divisor
    top = jnp.max(scores, axis=1, keepdims=True)
    grown = jnp.exp(scores - top)
    rise[...] = grown
    peak[...] = jnp.broadcast_to(top, peak.shape)
    lse_s = top + jnp.log(jnp.sum(grown, axis=1, keepdims=True))
    target = mentor[...].astype(f32) / sharpness_divisor
    cross = jnp.sum(prob[...] * (target - scores), axis=1, keepdims=True)
    lane = lax.broadcasted_iota(jnp.int32, (ROWS, 128), 1)
    columns = jnp.where(lane == 0, lse_s, jnp.where(lane == 1, lse_t[...], cross))
    flat = jnp.transpose(columns)
    lines = [flat[i : i + 1, h * 128 : (h + 1) * 128] for i in range(3) for h in range(2)]
    stats[...] = jnp.concatenate(lines, axis=0)


def as_columns(first, second):
    lines = [jnp.concatenate([v[0:1], v[1:2]], axis=1) for v in (first, second)]
    flat = jnp.transpose(jnp.concatenate(lines * 4, axis=0))
    return flat[:, 0:1], flat[:, 1:2]


def merged(parts):
    top = jnp.max(parts, axis=0)
    weight = jnp.exp(parts - top[None])
    total = jnp.sum(weight, axis=0)
    lse = top + jnp.log(total)
    cross = jnp.sum(weight[:, 2:4] * parts[:, 4:6], axis=0) / total[2:4]
    return lse[0:2], lse[2:4], cross


def merge_kernel(first, second, third, fourth, stats):
    all_s, all_t, cross = merged(jnp.stack([r[...] for r in (first, second, third, fourth)]))
    chunk = jnp.concatenate([all_s, all_t, cross], axis=0)
    stats[...] = jnp.broadcast_to(chunk[None], stats.shape)


def times_head(own, core, column, head, score_t, outs):
    for offset, back, ref in outs:
        j = lax.rem(column[0] - back + 4, 4)
        bases = [column_of(own, core, offset, j, odd) * SLAB for odd in range(2)]
        eighths = [head[pl.ds(pl.multiple_of(bases[z % 2] + 32 * z, 32), 32)] for z in range(NZ)]
        rows = jnp.concatenate(eighths, axis=0)
        ref[...] = jnp.dot(rows, score_t, preferred_element_type=f32).astype(ref.dtype)


def score_kernel(own, core, column, rise, peak, prob, lse_t, stats, head, score, score_t, b, c, mismatch):
    all_s, all_t, cross = merged(stats[...])
    mismatch[...] = sharpness_divisor * sharpness_divisor * (cross + all_s - all_t)
    end_s, end_t = as_columns(all_s, all_t)
    scale = objective_factor * sharpness_divisor
    share_s = scale * jnp.exp(peak[:, 0:1] - end_s)
    share_t = scale * jnp.exp(lse_t[:, 0:1] - end_t)
    rounded = (rise[...] * share_s - prob[...] * share_t).astype(bf16)
    score[...] = rounded
    score_t[...] = jnp.transpose(rounded)
    outs = [(o, j, r.at[pl.ds(j * SLAB, SLAB)]) for o, r in ((1, b), (3, c)) for j in range(4)]
    times_head(own, core, column, head, score_t[...], outs)


def rest_kernel(own, core, column, score_t, head, d0, d1, a):
    outs = [(2, j, (d0, d1)[j // 2].at[pl.ds((j % 2) * SLAB, SLAB)]) for j in range(4)]
    outs += [(0, j, a.at[pl.ds(j * SLAB, SLAB)]) for j in range(4)]
    times_head(own, core, column, head, score_t[...], outs)


def own_weight_kernel(mine, score, total):
    total[...] = jnp.dot(mine[...], score[...], preferred_element_type=f32)


def weight_kernel(own_total, theirs, score_theirs, out, held, sems):
    def send(i):
        return pltpu.make_async_copy(held.at[i], out.at[pl.ds(i * SLAB, SLAB)], sems.at[i])

    for i in range(8):
        rows = pl.ds(i * SLAB, SLAB)
        total = jnp.dot(theirs[rows], score_theirs[...], preferred_element_type=f32)
        held[i] = (own_total[rows] + total).astype(bf16)
        send(i).start()
    for i in range(8):
        send(i).wait()


def stats_of_all(stats):
    near = [stats, step(stats, 1, 0, 0), step(stats, -1, 0, 0), step(stats, 0, 0, 1)]
    (stats,) = call(
        merge_kernel, [((32, 6, 128), f32)], [("v", value) for value in near], 1000, 1000
    )
    return trade(stats, class_groups)


def shards(hidden, head_weight, mentor_outputs):
    here = lax.axis_index("vocab")
    core = lax.axis_index("rows").astype(jnp.int32)
    x, y = lax.rem(lax.div(here, NZ), NX), lax.div(here, NZ * NX)
    own = lax.rem(jnp.where(core == 0, x, y) + 2 * lax.rem(here, NZ), 4).astype(jnp.int32)[None]
    core = core[None]

    column = jnp.where(core[0] == 0, y, x).astype(jnp.int32)[None]
    a = class_of(hidden.T)
    prob, lse_t = call(
        target_kernel,
        [((ROWS, COLS), f32), ((ROWS, 128), f32)],
        [("v", mentor_outputs), ("v", head_weight)],
        10 * ROWS * COLS,
        2 * MIB,
    )
    b, c = step(a, -1, 0, 0), step(a, 1, 0, 0)
    d0, d1 = step(a[:512], 0, 0, 1), step(a[512:], 0, 0, -1)

    rise, peak, stats, mine, theirs = call(
        student_kernel,
        [((ROWS, COLS), f32), ((ROWS, 128), f32), ((6, 128), f32)] + [((FULL // 2, ROWS), bf16)] * 2,
        [("s", own), ("s", core), ("s", column), ("v", a), ("v", b), ("v", c), ("v", d0), ("v", d1), ("v", head_weight)]
        + [("v", mentor_outputs), ("v", prob), ("v", lse_t)],
        2 * FULL * ROWS * COLS,
        12 * MIB,
    )
    stats = stats_of_all(stats)

    score, score_t, b, c, mismatch = call(
        score_kernel,
        [((ROWS, COLS), bf16), ((COLS, ROWS), bf16)] + [((1024, ROWS), bf16)] * 2 + [((2, 128), f32)],
        [("s", own), ("s", core), ("s", column), ("v", rise), ("v", peak), ("v", prob), ("v", lse_t), ("v", stats), ("v", head_weight)],
        FULL * ROWS * COLS,
        8 * MIB,
    )
    b, c = step(b, 1, 0, 0), step(c, -1, 0, 0)
    d0, d1, a = call(
        rest_kernel,
        [((512, ROWS), bf16), ((512, ROWS), bf16), ((1024, ROWS), f32)],
        [("s", own), ("s", core), ("s", column), ("v", score_t), ("v", head_weight)],
        FULL * ROWS * COLS,
        7 * MIB,
    )
    d0, d1 = step(d0, 0, 0, 1), step(d1, 0, 0, -1)
    (own_total,) = call(
        own_weight_kernel,
        [((FULL // 2, COLS), f32)],
        [("v", mine), ("v", score)],
        FULL * ROWS * COLS,
        9 * MIB,
    )
    b, c, d0, d1, own_total = lax.optimization_barrier((b, c, d0, d1, own_total))
    part = a + b.astype(f32) + c.astype(f32) + jnp.concatenate([d0, d1], axis=0).astype(f32)
    part, theirs, score_theirs = lax.optimization_barrier((part, theirs, score))
    slabs = [part[i * SLAB : (i + 1) * SLAB] for i in range(4)]
    arrived = [step(slabs[i].astype(bf16), 0, -i, 0) for i in (1, 2, 3)]
    theirs, score_theirs = other_core(theirs), other_core(score_theirs)
    (weight_grad,) = call(
        weight_kernel,
        [((FULL // 2, COLS), bf16)],
        [("v", own_total), ("v", theirs), ("v", score_theirs)],
        FULL * ROWS * COLS,
        7 * MIB,
        [pltpu.VMEM((8, SLAB, COLS), bf16), pltpu.SemaphoreType.DMA((8,))],
        into="h",
    )
    *arrived, weight_grad = lax.optimization_barrier((*arrived, weight_grad))
    total = slabs[0]
    for value in arrived:
        total += value.astype(f32)
    total = trade(total.astype(bf16).reshape(NZ, 32, ROWS), octets)
    hidden_grad = jnp.sum(total.astype(f32), axis=0).astype(bf16).T
    return (hidden_grad, weight_grad, mismatch.reshape(ROWS))


def solution(mesh):
    return jax.shard_map(
        shards,
        mesh=mesh,
        in_specs=(P("rows", "vocab"), P(None, "vocab"), P("rows", "vocab")),
        out_specs=(P("rows", "vocab"), P("rows", "vocab"), P("rows")),
        check_vma=False,
    )
```
